256 devices in a mesh: mat: 4 (over x_lo, core), row: 16 (over x_hi, z), col: 4 (over y).
Axes of the slice: x: 4 (x_hi: 2, x_lo: 2; x = x_hi * 2 + x_lo), y: 4, z: 8, core: 2. Of those that a mesh axis runs over, the one named last changes fastest.
Arguments:
- iterate: bfloat16 [14336, 9216], P(('mat', 'row', 'col')), parts along dimension 0, may hold values from -0.043701172 to 0.043701172
Outputs:
- next_iterate: bfloat16 [14336, 9216], P(('mat', 'row', 'col')), parts along dimension 0
The draws below stay inside these ranges and needn't reach their ends.
There are 4 independent parts, one for each index of `mat`. The reference program is written for one: setup_inputs(seed, part) draws one part's arguments, and reference() takes and returns one part's arrays. A program takes and returns all parts, laid end to end along the dimension named above; each array names one. Nothing has to cross between parts.
All inputs are finite; a program needn't handle non-finite values.
Results may differ from the reference program's by a relative error of at most 0.006.
Values may be sent and summed in bfloat16 or wider, within the bound.
No kernel may reach another device: no remote copies, remote signals or barrier semaphores. Data moves between devices by JAX's collectives and lax.ppermute only.
A program may use at most 128 MiB of HBM per device.

```python
import math
import jax
import jax.numpy as jnp

ROWS = 3584
COLS = 9216


def level_of(own_key, shape, pieces, smallest, top_value):
    def one(position, shards_of):
        steps = jax.random.uniform(jax.random.fold_in(jax.random.fold_in(own_key, 6), position), (shards_of,), jnp.float32, smallest / len(pieces), top_value / len(pieces))
        return jnp.repeat(jnp.exp(steps), shape[position] // shards_of).reshape((-1,) + (1,) * (len(shape) - position - 1))

    level = one(*pieces[0])
    for cut in pieces[1:]:
        level = level * one(*cut)
    return level


def scatter_about(rng, shape, width, bound, split=(), held_as=jnp.bfloat16):
    drawn = width * jax.random.normal(rng, shape, jnp.float32)
    if split:
        drawn = drawn * level_of(rng, shape, split, -0.22, 0.18)
    return jnp.clip(drawn, -bound, bound).astype(held_as)


def setup_inputs(seed: int = 0, part: int = 0) -> dict:
    splits = jax.random.split(jax.random.key(seed), 2)
    own_keys = jax.random.split(jax.random.fold_in(splits[1], part), 2)
    return {
        "iterate": scatter_about(own_keys[0], (ROWS, COLS), (0.7 / COLS ** 0.5), 0.043701172, ((0, 64),)),
    }


def reference(iterate):
    gram_matrix = jnp.dot(iterate, iterate.T, preferred_element_type=jnp.float32).astype(jnp.bfloat16)
    squared = jnp.dot(gram_matrix, gram_matrix, preferred_element_type=jnp.float32)
    polynomial = (-4.775 * gram_matrix.astype(jnp.float32) + 2.0315 * squared).astype(jnp.bfloat16)
    product = jnp.dot(polynomial, iterate, preferred_element_type=jnp.float32)
    update = 3.4445 * iterate.astype(jnp.float32) + product
    return (math.sqrt(COLS) * update).astype(jnp.bfloat16)
```

```python
import math

import jax
import jax.numpy as jnp
from jax import lax
from jax.sharding import PartitionSpec as P

COLS = 9216
SPLIT = 5120
NX, NZ, NY = 2, 8, 4
F32, BF16 = jnp.float32, jnp.bfloat16


def z_shift(value, step):
    pairs = [(x * NZ + z, x * NZ + (z + step) % NZ) for x in range(NX) for z in range(NZ)]
    return lax.ppermute(value, "row", pairs)


def x_swap(value):
    pairs = [(x * NZ + z, (1 - x) * NZ + z) for x in range(NX) for z in range(NZ)]
    return lax.ppermute(value, "row", pairs)


def y_shift(value, step):
    return lax.ppermute(value, "col", [(y, (y + step) % NY) for y in range(NY)])


def ring_gather(block, shift, n):
    half = block.shape[1] // 2
    blocks = {0: block}
    ahead = behind = block
    for step in range(1, n // 2):
        ahead, behind = shift(ahead, -1), shift(behind, 1)
        blocks[step], blocks[n - step] = ahead, behind
    left, right = shift(ahead[:, :half], -1), shift(behind[:, half:], 1)
    blocks[n // 2] = (left, right)
    return blocks


def place(buffer, block, index):
    if isinstance(block, tuple):
        left, right = block
        buffer = lax.dynamic_update_slice(buffer, left[None], (index, 0, 0))
        return lax.dynamic_update_slice(buffer, right[None], (index, 0, left.shape[1]))
    return lax.dynamic_update_slice(buffer, block[None], (index, 0, 0))


def ring_reduce(part, shift, n):
    def add(term, got):
        return (term.astype(F32) + got.astype(F32)).astype(BF16)

    far = part(n // 2)
    half = far.shape[1] // 2
    up, down = shift(far[:, :half], 1), shift(far[:, half:], -1)
    for step in range(n // 2 - 1, 0, -1):
        a, b = part(step), part(n - step)
        if step == n // 2 - 1:
            a = jnp.concatenate([add(a[:, :half], up), a[:, half:]], 1)
            b = jnp.concatenate([b[:, :half], add(b[:, half:], down)], 1)
        else:
            a, b = add(a, up), add(b, down)
        up, down = shift(a, 1), shift(b, -1)
    return part(0).astype(F32) + up.astype(F32) + down.astype(F32)


def body(iterate):
    row = lax.axis_index("row")
    x, z, y = row // NZ, row % NZ, lax.axis_index("col")
    rows = iterate.shape[0]

    def z_at(k):
        return (z + k) % NZ

    def c_at(dx, dy):
        return ((x + dx) % NX) * NY + (y + dy) % NY

    def gather_z(block):
        return [(z_at(k), v) for k, v in ring_gather(block, z_shift, NZ).items()]

    def gather_c(block):
        other = x_swap(block)
        out = [(c_at(0, k), v) for k, v in ring_gather(block, y_shift, NY).items()]
        return out + [(c_at(1, k), v) for k, v in ring_gather(other, y_shift, NY).items()]

    by_z = jnp.zeros((NZ, rows, COLS), BF16)
    for index, block in gather_z(iterate):
        by_z = place(by_z, block, index)
    by_c = jnp.zeros((NX * NY, rows, COLS), BF16)
    for index, block in gather_c(iterate):
        by_c = place(by_c, block, index)
    side = NZ * rows
    by_z, by_c = by_z.reshape(side, COLS), by_c.reshape(side, COLS)

    gram_f32 = jnp.einsum("rk,ck->rc", by_c, by_z, preferred_element_type=F32)
    gram = gram_f32.astype(BF16)
    gram_t = gram.T

    left = jnp.zeros((NX * NY, side, side), BF16)
    for index, block in gather_c(gram_t):
        left = place(left, block, index)
    right = jnp.zeros((NX * NY, NZ, rows, side), BF16)
    for index, block in gather_z(gram):
        if isinstance(block, tuple):
            block = jnp.concatenate(block, 1)
        block = block.reshape(NX * NY, 1, rows, side)
        right = lax.dynamic_update_slice(right, block, (0, index, 0, 0))
    full = NZ * side
    squared = jnp.einsum(
        "lr,lc->rc", left.reshape(full, side), right.reshape(full, side), preferred_element_type=F32
    )
    polynomial = (-4.775 * gram.astype(F32) + 2.0315 * squared).astype(BF16)

    for_c = jnp.dot(polynomial, by_z[:, :SPLIT], preferred_element_type=F32).astype(BF16)
    for_c = for_c.reshape(NX * NY, rows, SPLIT)
    for_z = jnp.dot(polynomial.T, by_c[:, SPLIT:], preferred_element_type=F32).astype(BF16)
    for_z = for_z.reshape(NZ, rows, COLS - SPLIT)

    def pick(value, index):
        return lax.dynamic_index_in_dim(value, index, 0, keepdims=False)

    away = ring_reduce(lambda k: pick(for_c, c_at(1, k)), y_shift, NY).astype(BF16)
    away = x_swap(away)
    sum_c = ring_reduce(lambda k: pick(for_c, c_at(0, k)), y_shift, NY) + away.astype(F32)
    sum_z = ring_reduce(lambda k: pick(for_z, z_at(k)), z_shift, NZ)
    update = 3.4445 * iterate.astype(F32) + jnp.concatenate([sum_c, sum_z], 1)
    return (math.sqrt(COLS) * update).astype(BF16)


def solution(mesh):
    return jax.shard_map(
        body,
        mesh=mesh,
        in_specs=(P(("mat", "row", "col"), None),),
        out_specs=P(("mat", "row", "col"), None),
        check_vma=False,
    )
```

```python
import math

import jax
import jax.numpy as jnp
from jax import lax
from jax.sharding import PartitionSpec as P

COLS = 9216
SPLIT = 5120
NX, NZ, NY = 2, 8, 4
F32, BF16 = jnp.float32, jnp.bfloat16


def z_shift(value, step):
    pairs = [(x * NZ + z, x * NZ + (z + step) % NZ) for x in range(NX) for z in range(NZ)]
    return lax.ppermute(value, "row", pairs)


def x_swap(value):
    pairs = [(x * NZ + z, (1 - x) * NZ + z) for x in range(NX) for z in range(NZ)]
    return lax.ppermute(value, "row", pairs)


def y_shift(value, step):
    return lax.ppermute(value, "col", [(y, (y + step) % NY) for y in range(NY)])


def ring_gather(block, shift, n):
    half = block.shape[1] // 2
    blocks = {0: block}
    ahead = behind = block
    for step in range(1, n // 2):
        ahead, behind = shift(ahead, -1), shift(behind, 1)
        blocks[step], blocks[n - step] = ahead, behind
    left, right = shift(ahead[:, :half], -1), shift(behind[:, half:], 1)
    blocks[n // 2] = (left, right)
    return blocks


def place(buffer, block, index):
    if isinstance(block, tuple):
        left, right = block
        buffer = lax.dynamic_update_slice(buffer, left[None], (index, 0, 0))
        return lax.dynamic_update_slice(buffer, right[None], (index, 0, left.shape[1]))
    return lax.dynamic_update_slice(buffer, block[None], (index, 0, 0))


def ring_reduce(part, shift, n):
    def add(term, got):
        return (term.astype(F32) + got.astype(F32)).astype(BF16)

    far = part(n // 2)
    half = far.shape[1] // 2
    up, down = shift(far[:, :half], 1), shift(far[:, half:], -1)
    for step in range(n // 2 - 1, 0, -1):
        a, b = part(step), part(n - step)
        if step == n // 2 - 1:
            a = jnp.concatenate([add(a[:, :half], up), a[:, half:]], 1)
            b = jnp.concatenate([b[:, :half], add(b[:, half:], down)], 1)
        else:
            a, b = add(a, up), add(b, down)
        up, down = shift(a, 1), shift(b, -1)
    return part(0).astype(F32) + up.astype(F32) + down.astype(F32)


def body(iterate):
    row = lax.axis_index("row")
    x, z, y = row // NZ, row % NZ, lax.axis_index("col")
    rows = iterate.shape[0]

    def z_at(k):
        return (z + k) % NZ

    def c_at(dx, dy):
        return ((x + dx) % NX) * NY + (y + dy) % NY

    def gather_z(block):
        return [(z_at(k), v) for k, v in ring_gather(block, z_shift, NZ).items()]

    def gather_c(block):
        other = x_swap(block)
        out = [(c_at(0, k), v) for k, v in ring_gather(block, y_shift, NY).items()]
        return out + [(c_at(1, k), v) for k, v in ring_gather(other, y_shift, NY).items()]

    by_z = jnp.zeros((NZ, rows, COLS), BF16)
    for index, block in gather_z(iterate):
        by_z = place(by_z, block, index)
    by_c = jnp.zeros((NX * NY, rows, COLS), BF16)
    for index, block in gather_c(iterate):
        by_c = place(by_c, block, index)
    side = NZ * rows
    by_z, by_c = by_z.reshape(side, COLS), by_c.reshape(side, COLS)

    gram_f32 = jnp.einsum("rk,ck->rc", by_c, by_z, preferred_element_type=F32)
    gram = gram_f32.astype(BF16)
    gram_t = gram.T

    left = jnp.zeros((NX * NY, side, side), BF16)
    for index, block in gather_c(gram_t):
        left = place(left, block, index)
    right = jnp.zeros((NZ, side, side), BF16)
    for index, block in gather_z(gram):
        right = place(right, block, index)
    full = NZ * side
    left, right = lax.optimization_barrier((left, right))
    right = right.reshape(NZ, NX * NY, rows, side).swapaxes(0, 1)
    squared = jnp.einsum(
        "lr,lc->rc", left.reshape(full, side), right.reshape(full, side), preferred_element_type=F32
    )
    polynomial = (-4.775 * gram.astype(F32) + 2.0315 * squared).astype(BF16)

    for_c = jnp.dot(polynomial, by_z[:, :SPLIT], preferred_element_type=F32).astype(BF16)
    for_c = for_c.reshape(NX * NY, rows, SPLIT)
    for_z = jnp.dot(polynomial.T, by_c[:, SPLIT:], preferred_element_type=F32).astype(BF16)
    for_z = for_z.reshape(NZ, rows, COLS - SPLIT)

    def pick(value, index):
        return lax.dynamic_index_in_dim(value, index, 0, keepdims=False)

    away = ring_reduce(lambda k: pick(for_c, c_at(1, k)), y_shift, NY).astype(BF16)
    away = x_swap(away)
    sum_c = ring_reduce(lambda k: pick(for_c, c_at(0, k)), y_shift, NY) + away.astype(F32)
    sum_z = ring_reduce(lambda k: pick(for_z, z_at(k)), z_shift, NZ)
    update = 3.4445 * iterate.astype(F32) + jnp.concatenate([sum_c, sum_z], 1)
    return (math.sqrt(COLS) * update).astype(BF16)


def solution(mesh):
    return jax.shard_map(
        body,
        mesh=mesh,
        in_specs=(P(("mat", "row", "col"), None),),
        out_specs=P(("mat", "row", "col"), None),
        check_vma=False,
    )
```

```python
import math

import jax
import jax.numpy as jnp
from jax import lax
from jax.sharding import PartitionSpec as P

COLS = 9216
SPLIT = 4096
NX, NZ, NY = 2, 8, 4
F32, BF16 = jnp.float32, jnp.bfloat16


def z_shift(value, step):
    pairs = [(x * NZ + z, x * NZ + (z + step) % NZ) for x in range(NX) for z in range(NZ)]
    return lax.ppermute(value, "row", pairs)


def x_swap(value):
    pairs = [(x * NZ + z, (1 - x) * NZ + z) for x in range(NX) for z in range(NZ)]
    return lax.ppermute(value, "row", pairs)


def y_shift(value, step):
    return lax.ppermute(value, "col", [(y, (y + step) % NY) for y in range(NY)])


def ring_gather(block, shift, n, axis):
    half = block.shape[axis] // 2
    blocks = {0: block}
    ahead = behind = block
    for step in range(1, n // 2):
        ahead, behind = shift(ahead, -1), shift(behind, 1)
        blocks[step], blocks[n - step] = ahead, behind
    left = shift(lax.slice_in_dim(ahead, 0, half, axis=axis), -1)
    right = shift(lax.slice_in_dim(behind, half, 2 * half, axis=axis), 1)
    blocks[n // 2] = (left, right)
    return blocks


def place(buffer, block, index, axis):
    if isinstance(block, tuple):
        left, right = block
        buffer = lax.dynamic_update_slice(buffer, left[None], (index, 0, 0))
        start = (index, left.shape[0], 0) if axis == 0 else (index, 0, left.shape[1])
        return lax.dynamic_update_slice(buffer, right[None], start)
    return lax.dynamic_update_slice(buffer, block[None], (index, 0, 0))


def body(iterate):
    row = lax.axis_index("row")
    x, z, y = row // NZ, row % NZ, lax.axis_index("col")
    rows = iterate.shape[0]
    side = NZ * rows
    full = NZ * side

    def z_at(k):
        return (z + k) % NZ

    def c_at(dx, dy):
        return ((x + dx) % NX) * NY + (y + dy) % NY

    def pick(value, index):
        return lax.dynamic_index_in_dim(value, index, 0, keepdims=False)

    by_z = jnp.zeros((NZ, rows, COLS), BF16)
    for k, block in ring_gather(iterate, z_shift, NZ, 1).items():
        by_z = place(by_z, block, z_at(k), 1)
    by_c = jnp.zeros((NX * NY, rows, COLS), BF16)
    for dx, start in enumerate((iterate, x_swap(iterate))):
        for k, block in ring_gather(start, y_shift, NY, 1).items():
            by_c = place(by_c, block, c_at(dx, k), 1)
    by_z, by_c = by_z.reshape(side, COLS), by_c.reshape(side, COLS)

    gram = jnp.einsum("rk,ck->rc", by_c, by_z, preferred_element_type=F32).astype(BF16)
    gram_t = gram.T

    left = jnp.zeros((NX * NY, side, side), BF16)
    for dx, start in enumerate((gram_t, x_swap(gram_t))):
        left = place(left, start, c_at(dx, 0), 0)
        for k in (1, 3, 2):
            left = place(left, y_shift(start, -k), c_at(dx, k), 0)
    right = jnp.zeros((NZ, side, side), BF16)
    for k, block in ring_gather(gram, z_shift, NZ, 0).items():
        right = place(right, block, z_at(k), 0)
    left, right = lax.optimization_barrier((left, right))
    right = right.reshape(NZ, NX * NY, rows, side).swapaxes(0, 1)
    squared = jnp.einsum(
        "lr,lc->rc", left.reshape(full, side), right.reshape(full, side), preferred_element_type=F32
    )
    polynomial = (-4.775 * gram.astype(F32) + 2.0315 * squared).astype(BF16)
    polynomial_t = polynomial.T

    def term_z(lhs):
        return jnp.dot(lhs, by_c[:, SPLIT:], preferred_element_type=F32).astype(BF16)

    def term_c(lhs):
        return jnp.dot(lhs, by_z[:, :SPLIT], preferred_element_type=F32).astype(BF16)

    def add(term, got):
        return (term.astype(F32) + got.astype(F32)).astype(BF16)

    far = NZ // 2
    far_rows = lax.dynamic_slice_in_dim(polynomial_t, z_at(far) * rows, rows, 0)
    far_term = term_z(far_rows)
    half = far_term.shape[1] // 2
    up, down = z_shift(far_term[:, :half], 1), z_shift(far_term[:, half:], -1)
    by_y = polynomial.reshape(NX, NY, rows, side)

    def both(k):
        lhs = lax.dynamic_index_in_dim(by_y, (y + k) % NY, 1, keepdims=False)
        lhs = jnp.where(x == 0, lhs, lhs[::-1])
        return term_c(lhs.reshape(NX * rows, side))

    got_c = [y_shift(both(k), k) for k in (2, 1, 3)]
    for_z = term_z(polynomial_t).reshape(NZ, rows, COLS - SPLIT)
    for step in range(far - 1, 0, -1):
        a, b = pick(for_z, z_at(step)), pick(for_z, z_at(-step))
        if step == far - 1:
            a = jnp.concatenate([add(a[:, :half], up), a[:, half:]], 1)
            b = jnp.concatenate([b[:, :half], add(b[:, half:], down)], 1)
        else:
            a, b = add(a, up), add(b, down)
        up, down = z_shift(a, 1), z_shift(b, -1)
    sum_z = pick(for_z, z).astype(F32) + up.astype(F32) + down.astype(F32)

    sum_c = both(0).astype(F32)
    for got in got_c:
        sum_c = sum_c + got.astype(F32)
    sum_c = sum_c[:rows] + x_swap(sum_c[rows:].astype(BF16)).astype(F32)
    update = 3.4445 * iterate.astype(F32) + jnp.concatenate([sum_c, sum_z], 1)
    return (math.sqrt(COLS) * update).astype(BF16)


def solution(mesh):
    return jax.shard_map(
        body,
        mesh=mesh,
        in_specs=(P(("mat", "row", "col"), None),),
        out_specs=P(("mat", "row", "col"), None),
        check_vma=False,
    )
```

```python
import math

import jax
import jax.numpy as jnp
from jax import lax
from jax.experimental import pallas as pl
from jax.experimental.pallas import tpu as pltpu
from jax.sharding import PartitionSpec as P

COLS = 9216
SPLIT = 4608
BLOCK = 1024
NX, NZ, NY = 2, 8, 4
F32, BF16 = jnp.float32, jnp.bfloat16


def z_shift(value, step):
    pairs = [(x * NZ + z, x * NZ + (z + step) % NZ) for x in range(NX) for z in range(NZ)]
    return lax.ppermute(value, "row", pairs)


def x_swap(value):
    pairs = [(x * NZ + z, (1 - x) * NZ + z) for x in range(NX) for z in range(NZ)]
    return lax.ppermute(value, "row", pairs)


def y_shift(value, step):
    return lax.ppermute(value, "col", [(y, (y + step) % NY) for y in range(NY)])


class Lane:
    def __init__(self):
        self.last = None

    def send(self, value, shift, *step):
        if self.last is not None:
            value, _ = lax.optimization_barrier((value, self.last))
        self.last = shift(value, *step)
        return self.last


def gather_z(block, axis):
    half = block.shape[axis] // 2
    blocks = {0: block}
    ahead = behind = block
    for step in range(1, NZ // 2):
        ahead, behind = z_shift(ahead, -1), z_shift(behind, 1)
        blocks[step], blocks[NZ - step] = ahead, behind
    left = z_shift(lax.slice_in_dim(ahead, 0, half, axis=axis), -1)
    right = z_shift(lax.slice_in_dim(behind, half, 2 * half, axis=axis), 1)
    blocks[NZ // 2] = (left, right)
    return blocks


def place(buffer, block, index, axis):
    if isinstance(block, tuple):
        left, right = block
        buffer = lax.dynamic_update_slice(buffer, left[None], (index, 0, 0))
        start = (index, left.shape[0], 0) if axis == 0 else (index, 0, left.shape[1])
        return lax.dynamic_update_slice(buffer, right[None], start)
    return lax.dynamic_update_slice(buffer, block[None], (index, 0, 0))


def gram_kernel(by_c, by_z, out, total):
    step = pl.program_id(0)

    @pl.when(step == 0)
    def _():
        total[...] = jnp.zeros_like(total)

    total[...] += lax.dot_general(
        by_c[...], by_z[...], (((1,), (1,)), ((), ())), preferred_element_type=F32
    )

    @pl.when(step == pl.num_programs(0) - 1)
    def _():
        out[...] = total[...].astype(BF16)


def gram_product(by_c, by_z):
    side = by_c.shape[0]
    block = pl.BlockSpec((side, BLOCK), lambda k: (0, k))
    return pl.pallas_call(
        gram_kernel,
        out_shape=jax.ShapeDtypeStruct((side, side), BF16),
        grid=(COLS // BLOCK,),
        in_specs=[block, block],
        out_specs=pl.BlockSpec((side, side), lambda k: (0, 0)),
        scratch_shapes=[pltpu.VMEM((side, side), F32)],
        compiler_params=pltpu.CompilerParams(vmem_limit_bytes=32 * 2**20),
    )(by_c, by_z)


def polynomial_kernel(order, gram, right, *refs):
    *left, out = refs
    total = -4.775 * gram[...].astype(F32)
    squared = jnp.zeros_like(total)
    for i, block in enumerate(left):
        squared += jnp.dot(block[...], right[order[i]], preferred_element_type=F32)
    out[...] = (total + 2.0315 * squared).astype(BF16)


def polynomial_product(order, gram, right, left):
    vmem = pl.BlockSpec(memory_space=pltpu.VMEM)
    return pl.pallas_call(
        polynomial_kernel,
        out_shape=jax.ShapeDtypeStruct(gram.shape, BF16),
        in_specs=[pl.BlockSpec(memory_space=pltpu.SMEM)] + [vmem] * (2 + len(left)),
        out_specs=vmem,
        compiler_params=pltpu.CompilerParams(vmem_limit_bytes=32 * 2**20),
    )(order, gram, right, *left)


def body(iterate):
    row = lax.axis_index("row")
    x, z, y = row // NZ, row % NZ, lax.axis_index("col")
    rows = iterate.shape[0]
    side = NZ * rows

    def z_at(k):
        return (z + k) % NZ

    def c_at(dx, dy):
        return ((x + dx) % NX) * NY + (y + dy) % NY

    def pick(value, index):
        return lax.dynamic_index_in_dim(value, index, 0, keepdims=False)

    plus, minus = Lane(), Lane()
    cut = COLS * 3 // 4
    other = plus.send(iterate, x_swap)
    own_a = minus.send(iterate, y_shift, -1)
    own_b = plus.send(iterate, y_shift, 1)
    other_a = minus.send(other, y_shift, -1)
    other_b = plus.send(other, y_shift, 1)
    own_l = minus.send(own_a[:, :cut], y_shift, -1)
    own_r = plus.send(own_b[:, cut:], y_shift, 1)
    other_l = minus.send(other_a[:, :cut], y_shift, -1)
    other_r = plus.send(other_b[:, cut:], y_shift, 1)
    by_z = jnp.zeros((NZ, rows, COLS), BF16)
    for k, block in gather_z(iterate, 1).items():
        by_z = place(by_z, block, z_at(k), 1)
    by_c = jnp.zeros((NX * NY, rows, COLS), BF16)
    for dx, blocks in enumerate(
        ((iterate, own_a, own_b, (own_l, own_r)), (other, other_a, other_b, (other_l, other_r)))
    ):
        for k, block in zip((0, 1, 3, 2), blocks):
            by_c = place(by_c, block, c_at(dx, k), 1)
    by_z, by_c = by_z.reshape(side, COLS), by_c.reshape(side, COLS)

    gram = gram_product(by_c, by_z)

    plus, minus = Lane(), Lane()
    other = plus.send(gram, x_swap)
    left = {(0, 0): gram, (1, 0): other}
    for k in (1, 3, 2):
        left[0, k] = minus.send(gram, y_shift, -k)
    left[1, 1] = minus.send(other, y_shift, -1)
    for k in (3, 2):
        left[1, k] = plus.send(other, y_shift, -k)
    right = jnp.zeros((NZ, side, side), BF16)
    for k, block in gather_z(gram, 0).items():
        right = place(right, block, z_at(k), 0)
    right = lax.optimization_barrier(right)
    right = right.reshape(NZ, NX * NY, rows, side).swapaxes(0, 1).reshape(NX * NY, side, side)
    order = jnp.stack([c_at(dx, k) for dx, k in left]).astype(jnp.int32)
    polynomial = polynomial_product(order, gram, right, list(left.values()))
    polynomial_t = polynomial.T

    def term_z(lhs):
        return jnp.dot(lhs, by_c[:, SPLIT:], preferred_element_type=F32).astype(BF16)

    def add(term, got):
        return (term.astype(F32) + got.astype(F32)).astype(BF16)

    far = NZ // 2
    far_rows = lax.dynamic_slice_in_dim(polynomial_t, z_at(far) * rows, rows, 0)
    far_term = term_z(far_rows)
    half = far_term.shape[1] // 2
    up, down = z_shift(far_term[:, :half], 1), z_shift(far_term[:, half:], -1)

    polynomial, _ = lax.optimization_barrier((polynomial, far_term))
    for_c = jnp.dot(polynomial, by_z[:, :SPLIT], preferred_element_type=F32).astype(BF16)
    polynomial_t, for_c = lax.optimization_barrier((polynomial_t, for_c))
    for_c = for_c.reshape(NX * NY, rows, SPLIT)
    for_z = term_z(polynomial_t).reshape(NZ, rows, COLS - SPLIT)

    def term_c(dx, k):
        return pick(for_c, c_at(dx, k))

    plus, minus = Lane(), Lane()
    away = [minus.send(term_c(1, 2), y_shift, 2), plus.send(term_c(1, 3), y_shift, -1)]
    away.append(minus.send(term_c(1, 1), y_shift, 1))
    near = [plus.send(term_c(0, 2), y_shift, 2)]
    sum_away = term_c(1, 0).astype(F32)
    for got in away:
        sum_away = sum_away + got.astype(F32)
    got_x = minus.send(sum_away.astype(BF16), x_swap)
    near.append(plus.send(term_c(0, 1), y_shift, 1))
    near.append(plus.send(term_c(0, 3), y_shift, -1))

    for step in range(far - 1, 0, -1):
        a, b = pick(for_z, z_at(step)), pick(for_z, z_at(-step))
        if step == far - 1:
            a = jnp.concatenate([add(a[:, :half], up), a[:, half:]], 1)
            b = jnp.concatenate([b[:, :half], add(b[:, half:], down)], 1)
        else:
            a, b = add(a, up), add(b, down)
        up, down = z_shift(a, 1), z_shift(b, -1)
    sum_z = pick(for_z, z).astype(F32) + up.astype(F32) + down.astype(F32)
    sum_c = term_c(0, 0).astype(F32) + got_x.astype(F32)
    for got in near:
        sum_c = sum_c + got.astype(F32)
    update = 3.4445 * iterate.astype(F32) + jnp.concatenate([sum_c, sum_z], 1)
    return (math.sqrt(COLS) * update).astype(BF16)


def solution(mesh):
    return jax.shard_map(
        body,
        mesh=mesh,
        in_specs=(P(("mat", "row", "col"), None),),
        out_specs=P(("mat", "row", "col"), None),
        check_vma=False,
    )
```

```python
import math

import jax
import jax.numpy as jnp
from jax import lax
from jax.experimental import pallas as pl
from jax.experimental.pallas import tpu as pltpu
from jax.sharding import PartitionSpec as P

COLS = 9216
GATHERED = 2304
SPLIT, OFFLOADED = 4096, 1536
NX, NZ, NY = 2, 8, 4
F32, BF16 = jnp.float32, jnp.bfloat16


def z_shift(value, step):
    pairs = [(x * NZ + z, x * NZ + (z + step) % NZ) for x in range(NX) for z in range(NZ)]
    return lax.ppermute(value, "row", pairs)


def x_swap(value):
    pairs = [(x * NZ + z, (1 - x) * NZ + z) for x in range(NX) for z in range(NZ)]
    return lax.ppermute(value, "row", pairs)


def y_shift(value, step):
    return lax.ppermute(value, "col", [(y, (y + step) % NY) for y in range(NY)])


Z_GROUPS = [[x * NZ + z for z in range(NZ)] for x in range(NX)]


def together(sends, after=None):
    values = [send[0] for send in sends]
    if after is not None:
        values, _ = lax.optimization_barrier((values, after))
    return [send[1](value, *send[2:]) for value, send in zip(values, sends)]


class Lane:
    def __init__(self):
        self.last = None

    def send(self, value, shift, *step):
        if self.last is not None:
            value, _ = lax.optimization_barrier((value, self.last))
        self.last = shift(value, *step)
        return self.last


def gather_z(block, axis):
    half = block.shape[axis] // 2
    blocks = {0: block}
    ahead = behind = block
    for step in range(1, NZ // 2):
        ahead, behind = z_shift(ahead, -1), z_shift(behind, 1)
        blocks[step], blocks[NZ - step] = ahead, behind
    left = z_shift(lax.slice_in_dim(ahead, 0, half, axis=axis), -1)
    right = z_shift(lax.slice_in_dim(behind, half, 2 * half, axis=axis), 1)
    blocks[NZ // 2] = (left, right)
    return blocks


def place(buffer, block, index, axis):
    if isinstance(block, tuple):
        left, right = block
        buffer = lax.dynamic_update_slice(buffer, left[None], (index, 0, 0))
        start = (index, left.shape[0], 0) if axis == 0 else (index, 0, left.shape[1])
        return lax.dynamic_update_slice(buffer, right[None], start)
    return lax.dynamic_update_slice(buffer, block[None], (index, 0, 0))


def gram_kernel(by_c, by_z, rest, out, total):
    step = pl.program_id(0)

    def product(right):
        return lax.dot_general(
            by_c[...], right, (((1,), (1,)), ((), ())), preferred_element_type=F32
        )

    @pl.when(step == 0)
    def _():
        total[...] = product(rest[...])

    @pl.when(step > 0)
    def _():
        total[...] += product(by_z[...])

    @pl.when(step == pl.num_programs(0) - 1)
    def _():
        out[...] = total[...].astype(BF16)


def gram_product(by_c, by_z, rest):
    side, width = rest.shape
    steps = by_c.shape[1] // width
    return pl.pallas_call(
        gram_kernel,
        out_shape=jax.ShapeDtypeStruct((side, side), BF16),
        grid=(steps,),
        in_specs=[
            pl.BlockSpec((side, width), lambda k: (0, (k + steps - 1) % steps)),
            pl.BlockSpec((side, width), lambda k: (0, jnp.maximum(k - 1, 0))),
            pl.BlockSpec((side, width), lambda k: (0, 0)),
        ],
        out_specs=pl.BlockSpec((side, side), lambda k: (0, 0)),
        scratch_shapes=[pltpu.VMEM((side, side), F32)],
        compiler_params=pltpu.CompilerParams(vmem_limit_bytes=32 * 2**20),
    )(by_c, by_z, rest)


def polynomial_kernel(order, gram, right, *refs):
    *left, out = refs
    total = -4.775 * gram[...].astype(F32)
    squared = jnp.zeros_like(total)
    for i, block in enumerate(left):
        squared += jnp.dot(block[...], right[order[i]], preferred_element_type=F32)
    out[...] = (total + 2.0315 * squared).astype(BF16)


def polynomial_product(order, gram, right, left):
    vmem = pl.BlockSpec(memory_space=pltpu.VMEM)
    return pl.pallas_call(
        polynomial_kernel,
        out_shape=jax.ShapeDtypeStruct(gram.shape, BF16),
        in_specs=[pl.BlockSpec(memory_space=pltpu.SMEM)] + [vmem] * (2 + len(left)),
        out_specs=vmem,
        compiler_params=pltpu.CompilerParams(vmem_limit_bytes=32 * 2**20),
    )(order, gram, right, *left)


def body(iterate):
    row = lax.axis_index("row")
    x, z, y = row // NZ, row % NZ, lax.axis_index("col")
    rows = iterate.shape[0]
    side = NZ * rows

    def z_at(k):
        return (z + k) % NZ

    def c_at(dx, dy):
        return ((x + dx) % NX) * NY + (y + dy) % NY

    def pick(value, index):
        return lax.dynamic_index_in_dim(value, index, 0, keepdims=False)

    plus, minus = Lane(), Lane()
    cut = COLS * 3 // 4
    other = plus.send(iterate, x_swap)
    own_a = minus.send(iterate, y_shift, -1)
    own_b = plus.send(iterate, y_shift, 1)
    other_a = minus.send(other, y_shift, -1)
    other_b = plus.send(other, y_shift, 1)
    own_l = minus.send(own_a[:, :cut], y_shift, -1)
    own_r = plus.send(own_b[:, cut:], y_shift, 1)
    other_l = minus.send(other_a[:, :cut], y_shift, -1)
    other_r = plus.send(other_b[:, cut:], y_shift, 1)
    main = COLS - GATHERED
    rest = lax.all_gather(
        iterate[:, main:], "row", axis_index_groups=Z_GROUPS, axis=0, tiled=True
    )
    by_z = jnp.zeros((NZ, rows, main), BF16)
    for k, block in gather_z(iterate[:, :main], 1).items():
        by_z = place(by_z, block, z_at(k), 1)
    by_c = jnp.zeros((NX * NY, rows, COLS), BF16)
    for dx, blocks in enumerate(
        ((iterate, own_a, own_b, (own_l, own_r)), (other, other_a, other_b, (other_l, other_r)))
    ):
        for k, block in zip((0, 1, 3, 2), blocks):
            by_c = place(by_c, block, c_at(dx, k), 1)
    by_z, by_c = by_z.reshape(side, main), by_c.reshape(side, COLS)

    gram = gram_product(by_c, by_z, rest)

    plus, minus = Lane(), Lane()
    other = plus.send(gram, x_swap)
    left = {(0, 0): gram, (1, 0): other}
    for k in (1, 3, 2):
        left[0, k] = minus.send(gram, y_shift, -k)
    left[1, 1] = minus.send(other, y_shift, -1)
    for k in (3, 2):
        left[1, k] = plus.send(other, y_shift, -k)
    right = jnp.zeros((NZ, side, side), BF16)
    for k, block in gather_z(gram, 0).items():
        right = place(right, block, z_at(k), 0)
    right = lax.optimization_barrier(right)
    right = right.reshape(NZ, NX * NY, rows, side).swapaxes(0, 1).reshape(NX * NY, side, side)
    order = jnp.stack([c_at(dx, k) for dx, k in left]).astype(jnp.int32)
    polynomial = polynomial_product(order, gram, right, list(left.values()))
    polynomial_t = polynomial.T

    def add(term, got):
        return (term.astype(F32) + got.astype(F32)).astype(BF16)

    far, whole = NZ // 2, COLS - OFFLOADED
    for_z = jnp.dot(polynomial_t, by_c[:, SPLIT:], preferred_element_type=F32).astype(BF16)
    sum_rest = lax.psum_scatter(
        for_z[:, whole - SPLIT :], "row", axis_index_groups=Z_GROUPS, scatter_dimension=0, tiled=True
    )
    for_z = for_z[:, : whole - SPLIT].reshape(NZ, rows, whole - SPLIT)
    polynomial, _ = lax.optimization_barrier((polynomial, for_z))
    for_c = jnp.dot(polynomial, by_z[:, :SPLIT], preferred_element_type=F32).astype(BF16)
    for_c = for_c.reshape(NX * NY, rows, SPLIT)

    def term_z(k):
        return pick(for_z, z_at(k))

    def term_c(dx, k):
        return pick(for_c, c_at(dx, k))

    far_term = term_z(far)
    half = far_term.shape[1] // 2
    up, down = together([(far_term[:, :half], z_shift, 1), (far_term[:, half:], z_shift, -1)])
    a, b = term_z(far - 1), term_z(1 - far)
    a = jnp.concatenate([add(a[:, :half], up), a[:, half:]], 1)
    b = jnp.concatenate([b[:, :half], add(b[:, half:], down)], 1)
    up, down, *away = sent = together(
        [(a, z_shift, 1), (b, z_shift, -1)]
        + [(term_c(1, k), y_shift, k) for k in (2, 1, 3)],
        [up, down],
    )
    sum_away = term_c(1, 0).astype(F32)
    for got in away:
        sum_away = sum_away + got.astype(F32)
    a, b = add(term_z(2), up), add(term_z(-2), down)
    up, down, got_x, near = sent = together(
        [(a, z_shift, 1), (b, z_shift, -1), (sum_away.astype(BF16), x_swap), (term_c(0, 2), y_shift, 2)],
        sent,
    )
    a, b = add(term_z(1), up), add(term_z(-1), down)
    up, down, near_up, near_down = together(
        [(a, z_shift, 1), (b, z_shift, -1), (term_c(0, 1), y_shift, 1), (term_c(0, 3), y_shift, -1)],
        sent,
    )
    sum_z = term_z(0).astype(F32) + up.astype(F32) + down.astype(F32)
    sum_c = term_c(0, 0).astype(F32)
    for got in (got_x, near, near_up, near_down):
        sum_c = sum_c + got.astype(F32)
    product = jnp.concatenate([sum_c, sum_z, sum_rest.astype(F32)], 1)
    return (math.sqrt(COLS) * (3.4445 * iterate.astype(F32) + product)).astype(BF16)


def solution(mesh):
    return jax.shard_map(
        body,
        mesh=mesh,
        in_specs=(P(("mat", "row", "col"), None),),
        out_specs=P(("mat", "row", "col"), None),
        check_vma=False,
    )
```

```python
import math

import jax
import jax.numpy as jnp
from jax import lax
from jax.experimental import pallas as pl
from jax.experimental.pallas import tpu as pltpu
from jax.sharding import PartitionSpec as P

COLS = 9216
SPLIT = 4608
BLOCK = 4608
NX, NZ, NY = 2, 8, 4
F32, BF16 = jnp.float32, jnp.bfloat16


def z_shift(value, step):
    pairs = [(x * NZ + z, x * NZ + (z + step) % NZ) for x in range(NX) for z in range(NZ)]
    return lax.ppermute(value, "row", pairs)


def x_swap(value):
    pairs = [(x * NZ + z, (1 - x) * NZ + z) for x in range(NX) for z in range(NZ)]
    return lax.ppermute(value, "row", pairs)


def y_shift(value, step):
    return lax.ppermute(value, "col", [(y, (y + step) % NY) for y in range(NY)])


def together(sends, after=None):
    values = [send[0] for send in sends]
    if after is not None:
        values, _ = lax.optimization_barrier((values, after))
    return [send[1](value, *send[2:]) for value, send in zip(values, sends)]


class Lane:
    def __init__(self):
        self.last = None

    def send(self, value, shift, *step):
        if self.last is not None:
            value, _ = lax.optimization_barrier((value, self.last))
        self.last = shift(value, *step)
        return self.last


def gather_z(block, axis):
    half = block.shape[axis] // 2
    blocks = {0: block}
    ahead = behind = block
    for step in range(1, NZ // 2):
        ahead, behind = z_shift(ahead, -1), z_shift(behind, 1)
        blocks[step], blocks[NZ - step] = ahead, behind
    left = z_shift(lax.slice_in_dim(ahead, 0, half, axis=axis), -1)
    right = z_shift(lax.slice_in_dim(behind, half, 2 * half, axis=axis), 1)
    blocks[NZ // 2] = (left, right)
    return blocks


def place(buffer, block, index, axis):
    if isinstance(block, tuple):
        left, right = block
        buffer = lax.dynamic_update_slice(buffer, left[None], (index, 0, 0))
        start = (index, left.shape[0], 0) if axis == 0 else (index, 0, left.shape[1])
        return lax.dynamic_update_slice(buffer, right[None], start)
    return lax.dynamic_update_slice(buffer, block[None], (index, 0, 0))


def gram_kernel(by_c, by_z, out, total):
    step = pl.program_id(0)

    @pl.when(step == 0)
    def _():
        total[...] = jnp.zeros_like(total)

    total[...] += lax.dot_general(
        by_c[...], by_z[...], (((1,), (1,)), ((), ())), preferred_element_type=F32
    )

    @pl.when(step == pl.num_programs(0) - 1)
    def _():
        out[...] = total[...].astype(BF16)


def gram_product(by_c, by_z):
    side = by_c.shape[0]
    block = pl.BlockSpec((side, BLOCK), lambda k: (0, k))
    return pl.pallas_call(
        gram_kernel,
        out_shape=jax.ShapeDtypeStruct((side, side), BF16),
        grid=(COLS // BLOCK,),
        in_specs=[block, block],
        out_specs=pl.BlockSpec((side, side), lambda k: (0, 0)),
        scratch_shapes=[pltpu.VMEM((side, side), F32)],
        compiler_params=pltpu.CompilerParams(vmem_limit_bytes=48 * 2**20),
    )(by_c, by_z)


def polynomial_kernel(order, gram, right, *refs):
    *left, out = refs
    total = -4.775 * gram[...].astype(F32)
    squared = jnp.zeros_like(total)
    for i, block in enumerate(left):
        squared += jnp.dot(block[...], right[order[i]], preferred_element_type=F32)
    out[...] = (total + 2.0315 * squared).astype(BF16)


def polynomial_product(order, gram, right, left):
    vmem = pl.BlockSpec(memory_space=pltpu.VMEM)
    return pl.pallas_call(
        polynomial_kernel,
        out_shape=jax.ShapeDtypeStruct(gram.shape, BF16),
        in_specs=[pl.BlockSpec(memory_space=pltpu.SMEM)] + [vmem] * (2 + len(left)),
        out_specs=vmem,
        compiler_params=pltpu.CompilerParams(vmem_limit_bytes=32 * 2**20),
    )(order, gram, right, *left)


def body(iterate):
    row = lax.axis_index("row")
    x, z, y = row // NZ, row % NZ, lax.axis_index("col")
    rows = iterate.shape[0]
    side = NZ * rows

    def z_at(k):
        return (z + k) % NZ

    def c_at(dx, dy):
        return ((x + dx) % NX) * NY + (y + dy) % NY

    def pick(value, index):
        return lax.dynamic_index_in_dim(value, index, 0, keepdims=False)

    plus, minus = Lane(), Lane()
    cut = COLS * 3 // 4
    other = plus.send(iterate, x_swap)
    own_a = minus.send(iterate, y_shift, -1)
    own_b = plus.send(iterate, y_shift, 1)
    other_a = minus.send(other, y_shift, -1)
    other_b = plus.send(other, y_shift, 1)
    own_l = minus.send(own_a[:, :cut], y_shift, -1)
    own_r = plus.send(own_b[:, cut:], y_shift, 1)
    other_l = minus.send(other_a[:, :cut], y_shift, -1)
    other_r = plus.send(other_b[:, cut:], y_shift, 1)
    by_z = jnp.zeros((NZ, rows, COLS), BF16)
    for k, block in gather_z(iterate, 1).items():
        by_z = place(by_z, block, z_at(k), 1)
    by_c = jnp.zeros((NX * NY, rows, COLS), BF16)
    for dx, blocks in enumerate(
        ((iterate, own_a, own_b, (own_l, own_r)), (other, other_a, other_b, (other_l, other_r)))
    ):
        for k, block in zip((0, 1, 3, 2), blocks):
            by_c = place(by_c, block, c_at(dx, k), 1)
    by_z, by_c = by_z.reshape(side, COLS), by_c.reshape(side, COLS)

    gram = gram_product(by_c, by_z)

    half = side // 2
    z1, z7, other, own1 = sent = together(
        [(gram, z_shift, -1), (gram, z_shift, 1), (gram, x_swap), (gram, y_shift, -1)]
    )
    z2, z6, own3, own2 = sent = together(
        [(z1, z_shift, -1), (z7, z_shift, 1), (gram, y_shift, 1), (gram, y_shift, 2)], sent
    )
    z3, z5, other1, other3 = sent = together(
        [(z2, z_shift, -1), (z6, z_shift, 1), (other, y_shift, -1), (other, y_shift, 1)], sent
    )
    low, high, other2 = together(
        [(z3[:half], z_shift, -1), (z5[half:], z_shift, 1), (other, y_shift, 2)], sent
    )
    left = {(0, 0): gram, (0, 1): own1, (0, 2): own2, (0, 3): own3}
    left |= {(1, 0): other, (1, 1): other1, (1, 2): other2, (1, 3): other3}
    right = jnp.zeros((NZ, side, side), BF16)
    for k, block in enumerate((gram, z1, z2, z3, (low, high), z5, z6, z7)):
        right = place(right, block, z_at(k), 0)
    right = lax.optimization_barrier(right)
    right = right.reshape(NZ, NX * NY, rows, side).swapaxes(0, 1).reshape(NX * NY, side, side)
    order = jnp.stack([c_at(dx, k) for dx, k in left]).astype(jnp.int32)
    polynomial = polynomial_product(order, gram, right, list(left.values()))
    polynomial_t = polynomial.T

    def add(term, got):
        return (term.astype(F32) + got.astype(F32)).astype(BF16)

    far = NZ // 2
    for_z = jnp.dot(polynomial_t, by_c[:, SPLIT:], preferred_element_type=F32).astype(BF16)
    polynomial, _ = lax.optimization_barrier((polynomial, for_z))
    for_z = for_z.reshape(NZ, rows, COLS - SPLIT)
    for_c = jnp.dot(polynomial, by_z[:, :SPLIT], preferred_element_type=F32).astype(BF16)
    for_c = for_c.reshape(NX * NY, rows, SPLIT)

    def term_z(k):
        return pick(for_z, z_at(k))

    def term_c(dx, k):
        return pick(for_c, c_at(dx, k))

    far_term = term_z(far)
    half = far_term.shape[1] // 2
    up, down = together([(far_term[:, :half], z_shift, 1), (far_term[:, half:], z_shift, -1)])
    a, b = term_z(far - 1), term_z(1 - far)
    a = jnp.concatenate([add(a[:, :half], up), a[:, half:]], 1)
    b = jnp.concatenate([b[:, :half], add(b[:, half:], down)], 1)
    up, down, *away = sent = together(
        [(a, z_shift, 1), (b, z_shift, -1)]
        + [(term_c(1, k), y_shift, k) for k in (2, 1, 3)],
        [up, down],
    )
    sum_away = term_c(1, 0).astype(F32)
    for got in away:
        sum_away = sum_away + got.astype(F32)
    a, b = add(term_z(2), up), add(term_z(-2), down)
    up, down, got_x, near1, near3 = sent = together(
        [(a, z_shift, 1), (b, z_shift, -1), (sum_away.astype(BF16), x_swap)]
        + [(term_c(0, k), y_shift, k) for k in (1, 3)],
        sent,
    )
    a, b = add(term_z(1), up), add(term_z(-1), down)
    up, down, near2 = together(
        [(a, z_shift, 1), (b, z_shift, -1), (term_c(0, 2), y_shift, 2)], sent
    )
    sum_z = term_z(0).astype(F32) + up.astype(F32) + down.astype(F32)
    sum_c = term_c(0, 0).astype(F32)
    for got in (got_x, near1, near3, near2):
        sum_c = sum_c + got.astype(F32)
    update = 3.4445 * iterate.astype(F32) + jnp.concatenate([sum_c, sum_z], 1)
    return (math.sqrt(COLS) * update).astype(BF16)


def solution(mesh):
    return jax.shard_map(
        body,
        mesh=mesh,
        in_specs=(P(("mat", "row", "col"), None),),
        out_specs=P(("mat", "row", "col"), None),
        check_vma=False,
    )
```

```python
import math

import jax
import jax.numpy as jnp
from jax import lax
from jax.experimental import pallas as pl
from jax.experimental.pallas import tpu as pltpu
from jax.sharding import PartitionSpec as P

COLS = 9216
SPLIT = 4096
GATHERED = 2304
NX, NZ, NY = 2, 8, 4
F32, BF16 = jnp.float32, jnp.bfloat16


def z_shift(value, step):
    pairs = [(x * NZ + z, x * NZ + (z + step) % NZ) for x in range(NX) for z in range(NZ)]
    return lax.ppermute(value, "row", pairs)


def x_swap(value):
    pairs = [(x * NZ + z, (1 - x) * NZ + z) for x in range(NX) for z in range(NZ)]
    return lax.ppermute(value, "row", pairs)


def y_shift(value, step):
    return lax.ppermute(value, "col", [(y, (y + step) % NY) for y in range(NY)])


Z_GROUPS = [[x * NZ + z for z in range(NZ)] for x in range(NX)]


def together(sends, after=None):
    values, _ = lax.optimization_barrier(([send[0] for send in sends], after))
    return [send[1](value, *send[2:]) for value, send in zip(values, sends)]


def place(buffer, block, index, axis):
    if isinstance(block, tuple):
        left, right = block
        buffer = lax.dynamic_update_slice(buffer, left[None], (index, 0, 0))
        start = (index, left.shape[0], 0) if axis == 0 else (index, 0, left.shape[1])
        return lax.dynamic_update_slice(buffer, right[None], start)
    return lax.dynamic_update_slice(buffer, block[None], (index, 0, 0))


def gram_kernel(by_c, by_z, rest, out, total):
    step = pl.program_id(0)

    def product(right):
        return lax.dot_general(
            by_c[...], right, (((1,), (1,)), ((), ())), preferred_element_type=F32
        )

    @pl.when(step == 0)
    def _():
        total[...] = product(rest[...])

    @pl.when(step > 0)
    def _():
        total[...] += product(by_z[...])

    @pl.when(step == pl.num_programs(0) - 1)
    def _():
        out[...] = total[...].astype(BF16)


def gram_product(by_c, by_z, rest):
    side, width = rest.shape
    steps = by_c.shape[1] // width
    return pl.pallas_call(
        gram_kernel,
        out_shape=jax.ShapeDtypeStruct((side, side), BF16),
        grid=(steps,),
        in_specs=[
            pl.BlockSpec((side, width), lambda k: (0, (k + steps - 1) % steps)),
            pl.BlockSpec((side, width), lambda k: (0, jnp.maximum(k - 1, 0))),
            pl.BlockSpec((side, width), lambda k: (0, 0)),
        ],
        out_specs=pl.BlockSpec((side, side), lambda k: (0, 0)),
        scratch_shapes=[pltpu.VMEM((side, side), F32)],
        compiler_params=pltpu.CompilerParams(vmem_limit_bytes=48 * 2**20),
    )(by_c, by_z, rest)


def polynomial_kernel(order, gram, right, *refs):
    *left, out = refs
    total = -4.775 * gram[...].astype(F32)
    squared = jnp.zeros_like(total)
    for i, block in enumerate(left):
        squared += jnp.dot(block[...], right[order[i]], preferred_element_type=F32)
    out[...] = (total + 2.0315 * squared).astype(BF16)


def polynomial_product(order, gram, right, left):
    vmem = pl.BlockSpec(memory_space=pltpu.VMEM)
    return pl.pallas_call(
        polynomial_kernel,
        out_shape=jax.ShapeDtypeStruct(gram.shape, BF16),
        in_specs=[pl.BlockSpec(memory_space=pltpu.SMEM)] + [vmem] * (2 + len(left)),
        out_specs=vmem,
        compiler_params=pltpu.CompilerParams(vmem_limit_bytes=32 * 2**20),
    )(order, gram, right, *left)


def body(iterate):
    row = lax.axis_index("row")
    x, z, y = row // NZ, row % NZ, lax.axis_index("col")
    rows = iterate.shape[0]
    side = NZ * rows

    def z_at(k):
        return (z + k) % NZ

    def c_at(dx, dy):
        return ((x + dx) % NX) * NY + (y + dy) % NY

    def pick(value, index):
        return lax.dynamic_index_in_dim(value, index, 0, keepdims=False)

    main = COLS - GATHERED
    rest = lax.all_gather(
        iterate[:, main:], "row", axis_index_groups=Z_GROUPS, axis=0, tiled=True
    )
    mine = iterate[:, :main]
    z1, z7, other, own1 = sent = together(
        [(mine, z_shift, -1), (mine, z_shift, 1), (iterate, x_swap), (iterate, y_shift, -1)]
    )
    z2, z6, own3, other1 = sent = together(
        [(z1, z_shift, -1), (z7, z_shift, 1), (iterate, y_shift, 1), (other, y_shift, -1)], sent
    )
    z3, z5, other3, own2 = sent = together(
        [(z2, z_shift, -1), (z6, z_shift, 1), (other, y_shift, 1), (own1, y_shift, -1)], sent
    )
    z4l, z4r, other2l, other2r = together(
        [
            (z3[:, : main // 2], z_shift, -1),
            (z5[:, main // 2 :], z_shift, 1),
            (other1[:, : COLS // 2], y_shift, -1),
            (other3[:, COLS // 2 :], y_shift, 1),
        ],
        sent,
    )
    by_z = jnp.zeros((NZ, rows, main), BF16)
    for k, block in enumerate((mine, z1, z2, z3, (z4l, z4r), z5, z6, z7)):
        by_z = place(by_z, block, z_at(k), 1)
    by_c = jnp.zeros((NX * NY, rows, COLS), BF16)
    for k, block in enumerate((iterate, own1, own2, own3)):
        by_c = place(by_c, block, c_at(0, k), 1)
    for k, block in enumerate((other, other1, (other2l, other2r), other3)):
        by_c = place(by_c, block, c_at(1, k), 1)
    by_z, by_c = by_z.reshape(side, main), by_c.reshape(side, COLS)

    gram = gram_product(by_c, by_z, rest)

    half = side // 2
    z1, z7, other, own1, own3 = sent = together(
        [(gram, z_shift, -1), (gram, z_shift, 1), (gram, x_swap), (gram, y_shift, -1), (gram, y_shift, 1)]
    )
    pair = jnp.stack([gram, other])
    z2, z6, other1, other3, pair2 = together(
        [(z1, z_shift, -1), (z7, z_shift, 1), (other, y_shift, -1), (other, y_shift, 1), (pair, y_shift, 2)],
        sent,
    )
    z3, z5 = z_shift(z2, -1), z_shift(z6, 1)
    low, high = z_shift(z3[:half], -1), z_shift(z5[half:], 1)
    left = {(0, 0): gram, (0, 1): own1, (0, 2): pair2[0], (0, 3): own3}
    left |= {(1, 0): other, (1, 1): other1, (1, 2): pair2[1], (1, 3): other3}
    right = jnp.zeros((NZ, side, side), BF16)
    for k, block in enumerate((gram, z1, z2, z3, (low, high), z5, z6, z7)):
        right = place(right, block, z_at(k), 0)
    right = lax.optimization_barrier(right)
    right = right.reshape(NZ, NX * NY, rows, side).swapaxes(0, 1).reshape(NX * NY, side, side)
    order = jnp.stack([c_at(dx, k) for dx, k in left]).astype(jnp.int32)
    polynomial = polynomial_product(order, gram, right, list(left.values()))
    polynomial_t = polynomial.T

    def add(term, got):
        return (term.astype(F32) + got.astype(F32)).astype(BF16)

    far = NZ // 2
    for_z = jnp.dot(polynomial_t, by_c[:, SPLIT:], preferred_element_type=F32).astype(BF16)
    polynomial, _ = lax.optimization_barrier((polynomial, for_z))
    for_z = for_z.reshape(NZ, rows, COLS - SPLIT)
    for_c = jnp.dot(polynomial, by_z[:, :SPLIT], preferred_element_type=F32).astype(BF16)
    for_c = for_c.reshape(NX, NY, rows, SPLIT)

    def term_z(k):
        return pick(for_z, z_at(k))

    def term_c(k):
        return lax.dynamic_index_in_dim(for_c, (y + k) % NY, 1, keepdims=False)

    far_term = term_z(far)
    half = far_term.shape[1] // 2
    up, down = z_shift(far_term[:, :half], 1), z_shift(far_term[:, half:], -1)
    got_c = [y_shift(term_c(k), k) for k in (2, 1, 3)]
    a, b = term_z(far - 1), term_z(1 - far)
    a = jnp.concatenate([add(a[:, :half], up), a[:, half:]], 1)
    b = jnp.concatenate([b[:, :half], add(b[:, half:], down)], 1)
    up, down = z_shift(a, 1), z_shift(b, -1)
    up, down = z_shift(add(term_z(2), up), 1), z_shift(add(term_z(-2), down), -1)
    sum_c = term_c(0).astype(F32)
    for got in got_c:
        sum_c = sum_c + got.astype(F32)
    away = pick(sum_c, 1 - x).astype(BF16)
    up, down, got_x = together(
        [(add(term_z(1), up), z_shift, 1), (add(term_z(-1), down), z_shift, -1), (away, x_swap)]
    )
    sum_z = term_z(0).astype(F32) + up.astype(F32) + down.astype(F32)
    sum_c = pick(sum_c, x) + got_x.astype(F32)
    update = 3.4445 * iterate.astype(F32) + jnp.concatenate([sum_c, sum_z], 1)
    return (math.sqrt(COLS) * update).astype(BF16)


def solution(mesh):
    return jax.shard_map(
        body,
        mesh=mesh,
        in_specs=(P(("mat", "row", "col"), None),),
        out_specs=P(("mat", "row", "col"), None),
        check_vma=False,
    )
```

```python
import math

import jax
import jax.numpy as jnp
from jax import lax
from jax.experimental import pallas as pl
from jax.experimental.pallas import tpu as pltpu
from jax.sharding import PartitionSpec as P

COLS = 9216
SPLIT = 4096
BLOCK = 4608
NX, NZ, NY = 2, 8, 4
F32, BF16 = jnp.float32, jnp.bfloat16


def z_shift(value, step):
    pairs = [(x * NZ + z, x * NZ + (z + step) % NZ) for x in range(NX) for z in range(NZ)]
    return lax.ppermute(value, "row", pairs)


def x_swap(value):
    pairs = [(x * NZ + z, (1 - x) * NZ + z) for x in range(NX) for z in range(NZ)]
    return lax.ppermute(value, "row", pairs)


def y_shift(value, step):
    return lax.ppermute(value, "col", [(y, (y + step) % NY) for y in range(NY)])


def together(sends, after=None):
    values, _ = lax.optimization_barrier(([send[0] for send in sends], after))
    return [send[1](value, *send[2:]) for value, send in zip(values, sends)]


class Lane:
    def __init__(self):
        self.last = None

    def send(self, value, shift, *step):
        if self.last is not None:
            value, _ = lax.optimization_barrier((value, self.last))
        self.last = shift(value, *step)
        return self.last


def gather_z(block, axis):
    half = block.shape[axis] // 2
    blocks = {0: block}
    ahead = behind = block
    for step in range(1, NZ // 2):
        ahead, behind = z_shift(ahead, -1), z_shift(behind, 1)
        blocks[step], blocks[NZ - step] = ahead, behind
    left = z_shift(lax.slice_in_dim(ahead, 0, half, axis=axis), -1)
    right = z_shift(lax.slice_in_dim(behind, half, 2 * half, axis=axis), 1)
    blocks[NZ // 2] = (left, right)
    return blocks


def place(buffer, block, index, axis):
    if isinstance(block, tuple):
        left, right = block
        buffer = lax.dynamic_update_slice(buffer, left[None], (index, 0, 0))
        start = (index, left.shape[0], 0) if axis == 0 else (index, 0, left.shape[1])
        return lax.dynamic_update_slice(buffer, right[None], start)
    return lax.dynamic_update_slice(buffer, block[None], (index, 0, 0))


def gram_kernel(by_c, by_z, out, total):
    step = pl.program_id(0)

    @pl.when(step == 0)
    def _():
        total[...] = jnp.zeros_like(total)

    total[...] += lax.dot_general(
        by_c[...], by_z[...], (((1,), (1,)), ((), ())), preferred_element_type=F32
    )

    @pl.when(step == pl.num_programs(0) - 1)
    def _():
        out[...] = total[...].astype(BF16)


def gram_product(by_c, by_z):
    side = by_c.shape[0]
    block = pl.BlockSpec((side, BLOCK), lambda k: (0, k))
    return pl.pallas_call(
        gram_kernel,
        out_shape=jax.ShapeDtypeStruct((side, side), BF16),
        grid=(COLS // BLOCK,),
        in_specs=[block, block],
        out_specs=pl.BlockSpec((side, side), lambda k: (0, 0)),
        scratch_shapes=[pltpu.VMEM((side, side), F32)],
        compiler_params=pltpu.CompilerParams(vmem_limit_bytes=48 * 2**20),
    )(by_c, by_z)


def polynomial_kernel(order, gram, right, *refs):
    *left, out = refs
    total = -4.775 * gram[...].astype(F32)
    squared = jnp.zeros_like(total)
    for i, block in enumerate(left):
        squared += jnp.dot(block[...], right[order[i]], preferred_element_type=F32)
    out[...] = (total + 2.0315 * squared).astype(BF16)


def polynomial_product(order, gram, right, left):
    vmem = pl.BlockSpec(memory_space=pltpu.VMEM)
    return pl.pallas_call(
        polynomial_kernel,
        out_shape=jax.ShapeDtypeStruct(gram.shape, BF16),
        in_specs=[pl.BlockSpec(memory_space=pltpu.SMEM)] + [vmem] * (2 + len(left)),
        out_specs=vmem,
        compiler_params=pltpu.CompilerParams(vmem_limit_bytes=32 * 2**20),
    )(order, gram, right, *left)


def body(iterate):
    row = lax.axis_index("row")
    x, z, y = row // NZ, row % NZ, lax.axis_index("col")
    rows = iterate.shape[0]
    side = NZ * rows

    def z_at(k):
        return (z + k) % NZ

    def c_at(dx, dy):
        return ((x + dx) % NX) * NY + (y + dy) % NY

    def pick(value, index):
        return lax.dynamic_index_in_dim(value, index, 0, keepdims=False)

    plus, minus = Lane(), Lane()
    cut = COLS * 3 // 4
    other = plus.send(iterate, x_swap)
    own_a = minus.send(iterate, y_shift, -1)
    own_b = plus.send(iterate, y_shift, 1)
    other_a = minus.send(other, y_shift, -1)
    other_b = plus.send(other, y_shift, 1)
    own_l = minus.send(own_a[:, :cut], y_shift, -1)
    own_r = plus.send(own_b[:, cut:], y_shift, 1)
    other_l = minus.send(other_a[:, :cut], y_shift, -1)
    other_r = plus.send(other_b[:, cut:], y_shift, 1)
    by_z = jnp.zeros((NZ, rows, COLS), BF16)
    for k, block in gather_z(iterate, 1).items():
        by_z = place(by_z, block, z_at(k), 1)
    by_c = jnp.zeros((NX * NY, rows, COLS), BF16)
    for dx, blocks in enumerate(
        ((iterate, own_a, own_b, (own_l, own_r)), (other, other_a, other_b, (other_l, other_r)))
    ):
        for k, block in zip((0, 1, 3, 2), blocks):
            by_c = place(by_c, block, c_at(dx, k), 1)
    by_z, by_c = by_z.reshape(side, COLS), by_c.reshape(side, COLS)

    gram = gram_product(by_c, by_z)

    half = side // 2
    z1, z7, other, own1, own3 = sent = together(
        [(gram, z_shift, -1), (gram, z_shift, 1), (gram, x_swap), (gram, y_shift, -1), (gram, y_shift, 1)]
    )
    pair = jnp.stack([gram, other])
    z2, z6, other1, other3, pair2 = together(
        [(z1, z_shift, -1), (z7, z_shift, 1), (other, y_shift, -1), (other, y_shift, 1), (pair, y_shift, 2)],
        sent,
    )
    z3, z5 = z_shift(z2, -1), z_shift(z6, 1)
    low, high = z_shift(z3[:half], -1), z_shift(z5[half:], 1)
    left = {(0, 0): gram, (0, 1): own1, (0, 2): pair2[0], (0, 3): own3}
    left |= {(1, 0): other, (1, 1): other1, (1, 2): pair2[1], (1, 3): other3}
    right = jnp.zeros((NZ, side, side), BF16)
    for k, block in enumerate((gram, z1, z2, z3, (low, high), z5, z6, z7)):
        right = place(right, block, z_at(k), 0)
    right = lax.optimization_barrier(right)
    right = right.reshape(NZ, NX * NY, rows, side).swapaxes(0, 1).reshape(NX * NY, side, side)
    order = jnp.stack([c_at(dx, k) for dx, k in left]).astype(jnp.int32)
    polynomial = polynomial_product(order, gram, right, list(left.values()))
    polynomial_t = polynomial.T

    def add(term, got):
        return (term.astype(F32) + got.astype(F32)).astype(BF16)

    far = NZ // 2
    for_z = jnp.dot(polynomial_t, by_c[:, SPLIT:], preferred_element_type=F32).astype(BF16)
    polynomial, _ = lax.optimization_barrier((polynomial, for_z))
    for_z = for_z.reshape(NZ, rows, COLS - SPLIT)
    for_c = jnp.dot(polynomial, by_z[:, :SPLIT], preferred_element_type=F32).astype(BF16)
    for_c = for_c.reshape(NX, NY, rows, SPLIT)

    def term_z(k):
        return pick(for_z, z_at(k))

    def term_c(k):
        return lax.dynamic_index_in_dim(for_c, (y + k) % NY, 1, keepdims=False)

    far_term = term_z(far)
    half = far_term.shape[1] // 2
    up, down = z_shift(far_term[:, :half], 1), z_shift(far_term[:, half:], -1)
    got_c = [y_shift(term_c(k), k) for k in (2, 1, 3)]
    a, b = term_z(far - 1), term_z(1 - far)
    a = jnp.concatenate([add(a[:, :half], up), a[:, half:]], 1)
    b = jnp.concatenate([b[:, :half], add(b[:, half:], down)], 1)
    a, b, _ = lax.optimization_barrier((a, b, for_c))
    up, down = z_shift(a, 1), z_shift(b, -1)
    up, down = z_shift(add(term_z(2), up), 1), z_shift(add(term_z(-2), down), -1)
    sum_c = term_c(0).astype(F32)
    for got in got_c:
        sum_c = sum_c + got.astype(F32)
    away = pick(sum_c, 1 - x).astype(BF16)
    up, down, got_x = together(
        [(add(term_z(1), up), z_shift, 1), (add(term_z(-1), down), z_shift, -1), (away, x_swap)]
    )
    sum_z = term_z(0).astype(F32) + up.astype(F32) + down.astype(F32)
    sum_c = pick(sum_c, x) + got_x.astype(F32)
    update = 3.4445 * iterate.astype(F32) + jnp.concatenate([sum_c, sum_z], 1)
    return (math.sqrt(COLS) * update).astype(BF16)


def solution(mesh):
    return jax.shard_map(
        body,
        mesh=mesh,
        in_specs=(P(("mat", "row", "col"), None),),
        out_specs=P(("mat", "row", "col"), None),
        check_vma=False,
    )
```

```python
import math

import jax
import jax.numpy as jnp
from jax import lax
from jax.experimental import pallas as pl
from jax.experimental.pallas import tpu as pltpu
from jax.sharding import PartitionSpec as P

COLS = 9216
SPLIT = 4096
BLOCK = 4608
FIRST = 256
NX, NZ, NY = 2, 8, 4
F32, BF16 = jnp.float32, jnp.bfloat16


def z_shift(value, step):
    pairs = [(x * NZ + z, x * NZ + (z + step) % NZ) for x in range(NX) for z in range(NZ)]
    return lax.ppermute(value, "row", pairs)


def x_swap(value):
    pairs = [(x * NZ + z, (1 - x) * NZ + z) for x in range(NX) for z in range(NZ)]
    return lax.ppermute(value, "row", pairs)


def y_shift(value, step):
    return lax.ppermute(value, "col", [(y, (y + step) % NY) for y in range(NY)])


def together(sends, after=None):
    values, _ = lax.optimization_barrier(([send[0] for send in sends], after))
    return [send[1](value, *send[2:]) for value, send in zip(values, sends)]


class Lane:
    def __init__(self):
        self.last = None

    def send(self, value, shift, *step):
        if self.last is not None:
            value, _ = lax.optimization_barrier((value, self.last))
        self.last = shift(value, *step)
        return self.last


def gather_z(block, axis):
    half = block.shape[axis] // 2
    blocks = {0: block}
    ahead = behind = block
    for step in range(1, NZ // 2):
        ahead, behind = z_shift(ahead, -1), z_shift(behind, 1)
        blocks[step], blocks[NZ - step] = ahead, behind
    left = z_shift(lax.slice_in_dim(ahead, 0, half, axis=axis), -1)
    right = z_shift(lax.slice_in_dim(behind, half, 2 * half, axis=axis), 1)
    blocks[NZ // 2] = (left, right)
    return blocks


def place(buffer, block, index, axis):
    if isinstance(block, tuple):
        left, right = block
        buffer = lax.dynamic_update_slice(buffer, left[None], (index, 0, 0))
        start = (index, left.shape[0], 0) if axis == 0 else (index, 0, left.shape[1])
        return lax.dynamic_update_slice(buffer, right[None], start)
    return lax.dynamic_update_slice(buffer, block[None], (index, 0, 0))


def gram_kernel(by_c, by_z, out, total):
    step = pl.program_id(0)

    @pl.when(step == 0)
    def _():
        total[...] = jnp.zeros_like(total)

    total[...] += lax.dot_general(
        by_c[...], by_z[...], (((1,), (1,)), ((), ())), preferred_element_type=F32
    )

    @pl.when(step == pl.num_programs(0) - 1)
    def _():
        out[...] = total[...].astype(BF16)


def gram_product(by_c, by_z):
    side = by_c.shape[0]
    block = pl.BlockSpec((side, BLOCK), lambda k: (0, k))
    return pl.pallas_call(
        gram_kernel,
        out_shape=jax.ShapeDtypeStruct((side, side), BF16),
        grid=(COLS // BLOCK,),
        in_specs=[block, block],
        out_specs=pl.BlockSpec((side, side), lambda k: (0, 0)),
        scratch_shapes=[pltpu.VMEM((side, side), F32)],
        compiler_params=pltpu.CompilerParams(vmem_limit_bytes=48 * 2**20),
    )(by_c, by_z)


def polynomial_kernel(order, gram, right, *refs):
    *left, out = refs
    total = -4.775 * gram[...].astype(F32)
    squared = jnp.zeros_like(total)
    for i, block in enumerate(left):
        squared += jnp.dot(block[...], right[order[i]], preferred_element_type=F32)
    out[...] = (total + 2.0315 * squared).astype(BF16)


def polynomial_product(order, gram, right, left):
    vmem = pl.BlockSpec(memory_space=pltpu.VMEM)
    return pl.pallas_call(
        polynomial_kernel,
        out_shape=jax.ShapeDtypeStruct(gram.shape, BF16),
        in_specs=[pl.BlockSpec(memory_space=pltpu.SMEM)] + [vmem] * (2 + len(left)),
        out_specs=vmem,
        compiler_params=pltpu.CompilerParams(vmem_limit_bytes=32 * 2**20),
    )(order, gram, right, *left)


def sum_kernel(index, mine, *refs):
    *got, near, away = refs
    x = index[0]

    def total(i):
        value = mine[i].astype(F32)
        for block in got:
            value += block[i].astype(F32)
        return value

    near[...] = total(x)
    away[...] = total(1 - x).astype(BF16)


def sum_blocks(x, mine, got):
    vmem = pl.BlockSpec(memory_space=pltpu.VMEM)
    shape = mine.shape[1:]
    return pl.pallas_call(
        sum_kernel,
        out_shape=[jax.ShapeDtypeStruct(shape, F32), jax.ShapeDtypeStruct(shape, BF16)],
        in_specs=[pl.BlockSpec(memory_space=pltpu.SMEM)] + [vmem] * (1 + len(got)),
        out_specs=[vmem, vmem],
        compiler_params=pltpu.CompilerParams(vmem_limit_bytes=32 * 2**20),
    )(x.reshape(1).astype(jnp.int32), mine, *got)


def body(iterate):
    row = lax.axis_index("row")
    x, z, y = row // NZ, row % NZ, lax.axis_index("col")
    rows = iterate.shape[0]
    side = NZ * rows

    def z_at(k):
        return (z + k) % NZ

    def c_at(dx, dy):
        return ((x + dx) % NX) * NY + (y + dy) % NY

    def pick(value, index):
        return lax.dynamic_index_in_dim(value, index, 0, keepdims=False)

    plus, minus = Lane(), Lane()
    cut = COLS * 3 // 4
    other = plus.send(iterate, x_swap)
    own_a = minus.send(iterate, y_shift, -1)
    own_b = plus.send(iterate, y_shift, 1)
    other_a = minus.send(other, y_shift, -1)
    other_b = plus.send(other, y_shift, 1)
    own_l = minus.send(own_a[:, :cut], y_shift, -1)
    own_r = plus.send(own_b[:, cut:], y_shift, 1)
    other_l = minus.send(other_a[:, :cut], y_shift, -1)
    other_r = plus.send(other_b[:, cut:], y_shift, 1)
    by_z = jnp.zeros((NZ, rows, COLS), BF16)
    for k, block in gather_z(iterate, 1).items():
        by_z = place(by_z, block, z_at(k), 1)
    by_c = jnp.zeros((NX * NY, rows, COLS), BF16)
    for dx, blocks in enumerate(
        ((iterate, own_a, own_b, (own_l, own_r)), (other, other_a, other_b, (other_l, other_r)))
    ):
        for k, block in zip((0, 1, 3, 2), blocks):
            by_c = place(by_c, block, c_at(dx, k), 1)
    by_z, by_c = by_z.reshape(side, COLS), by_c.reshape(side, COLS)

    gram = gram_product(by_c, by_z)

    half = side // 2
    z1, z7, other, own1, own3 = sent = together(
        [(gram, z_shift, -1), (gram, z_shift, 1), (gram, x_swap), (gram, y_shift, -1), (gram, y_shift, 1)]
    )
    pair = jnp.stack([gram, other])
    z2, z6, other1, other3, pair2 = together(
        [(z1, z_shift, -1), (z7, z_shift, 1), (other, y_shift, -1), (other, y_shift, 1), (pair, y_shift, 2)],
        sent,
    )
    z3, z5 = z_shift(z2, -1), z_shift(z6, 1)
    low, high = z_shift(z3[:half], -1), z_shift(z5[half:], 1)
    left = {(0, 0): gram, (0, 1): own1, (0, 2): pair2[0], (0, 3): own3}
    left |= {(1, 0): other, (1, 1): other1, (1, 2): pair2[1], (1, 3): other3}
    right = jnp.zeros((NZ, side, side), BF16)
    for k, block in enumerate((gram, z1, z2, z3, (low, high), z5, z6, z7)):
        right = place(right, block, z_at(k), 0)
    right = lax.optimization_barrier(right)
    right = right.reshape(NZ, NX * NY, rows, side).swapaxes(0, 1).reshape(NX * NY, side, side)
    order = jnp.stack([c_at(dx, k) for dx, k in left]).astype(jnp.int32)
    polynomial = polynomial_product(order, gram, right, list(left.values()))
    polynomial_t = polynomial.T

    def add(term, got):
        return (term.astype(F32) + got.astype(F32)).astype(BF16)

    far = NZ // 2
    for_z = jnp.dot(polynomial_t, by_c[:, SPLIT:], preferred_element_type=F32).astype(BF16)
    polynomial, _ = lax.optimization_barrier((polynomial, for_z))
    for_z = for_z.reshape(NZ, rows, COLS - SPLIT)
    for_c = jnp.dot(polynomial, by_z[:, :SPLIT], preferred_element_type=F32).astype(BF16)
    for_c = for_c.reshape(NX, NY, rows, SPLIT)

    def term_z(k):
        return pick(for_z, z_at(k))

    def term_c(k):
        return lax.dynamic_index_in_dim(for_c, (y + k) % NY, 1, keepdims=False)

    far_term = term_z(far)
    half = far_term.shape[1] // 2
    up, down = z_shift(far_term[:, :half], 1), z_shift(far_term[:, half:], -1)
    got_c = [y_shift(term_c(k), k) for k in (2, 1, 3)]
    a, b = term_z(far - 1), term_z(1 - far)
    a = jnp.concatenate([add(a[:, :half], up), a[:, half:]], 1)
    b = jnp.concatenate([b[:, :half], add(b[:, half:], down)], 1)
    a, b, _ = lax.optimization_barrier((a, b, for_c))
    up, down = z_shift(a, 1), z_shift(b, -1)
    up, down = together(
        [(add(term_z(2), up), z_shift, 1), (add(term_z(-2), down), z_shift, -1)], (up, down)
    )
    sum_c, away = sum_blocks(x, term_c(0), got_c)
    up, down = together(
        [(add(term_z(1), up), z_shift, 1), (add(term_z(-1), down), z_shift, -1)], (up, down)
    )
    first = x_swap(away[:, :FIRST])
    second, _ = lax.optimization_barrier((away[:, FIRST:], first))
    got_x = jnp.concatenate([first, x_swap(second)], 1)
    sum_z = term_z(0).astype(F32) + up.astype(F32) + down.astype(F32)
    sum_c = sum_c + got_x.astype(F32)
    update = 3.4445 * iterate.astype(F32) + jnp.concatenate([sum_c, sum_z], 1)
    return (math.sqrt(COLS) * update).astype(BF16)


def solution(mesh):
    return jax.shard_map(
        body,
        mesh=mesh,
        in_specs=(P(("mat", "row", "col"), None),),
        out_specs=P(("mat", "row", "col"), None),
        check_vma=False,
    )
```

```python
import math

import jax
import jax.numpy as jnp
from jax import lax
from jax.experimental import pallas as pl
from jax.experimental.pallas import tpu as pltpu
from jax.sharding import PartitionSpec as P

COLS = 9216
SPLIT = 4096
FIRST = 3840
NX, NZ, NY = 2, 8, 4
F32, BF16 = jnp.float32, jnp.bfloat16


def z_shift(value, step):
    pairs = [(x * NZ + z, x * NZ + (z + step) % NZ) for x in range(NX) for z in range(NZ)]
    return lax.ppermute(value, "row", pairs)


def x_swap(value):
    pairs = [(x * NZ + z, (1 - x) * NZ + z) for x in range(NX) for z in range(NZ)]
    return lax.ppermute(value, "row", pairs)


def y_shift(value, step):
    return lax.ppermute(value, "col", [(y, (y + step) % NY) for y in range(NY)])


def together(sends, after=None):
    values, _ = lax.optimization_barrier(([send[0] for send in sends], after))
    return [send[1](value, *send[2:]) for value, send in zip(values, sends)]


class Lane:
    def __init__(self):
        self.last = None

    def send(self, value, shift, *step):
        if self.last is not None:
            value, _ = lax.optimization_barrier((value, self.last))
        self.last = shift(value, *step)
        return self.last


def gather_z(block, axis):
    half = block.shape[axis] // 2
    blocks = {0: block}
    ahead = behind = block
    for step in range(1, NZ // 2):
        ahead, behind = z_shift(ahead, -1), z_shift(behind, 1)
        blocks[step], blocks[NZ - step] = ahead, behind
    left = z_shift(lax.slice_in_dim(ahead, 0, half, axis=axis), -1)
    right = z_shift(lax.slice_in_dim(behind, half, 2 * half, axis=axis), 1)
    blocks[NZ // 2] = (left, right)
    return blocks


def place(buffer, block, index, axis):
    if isinstance(block, tuple):
        left, right = block
        buffer = lax.dynamic_update_slice(buffer, left[None], (index, 0, 0))
        start = (index, left.shape[0], 0) if axis == 0 else (index, 0, left.shape[1])
        return lax.dynamic_update_slice(buffer, right[None], start)
    return lax.dynamic_update_slice(buffer, block[None], (index, 0, 0))


def gram_kernel(by_c, by_z, out):
    out[...] = lax.dot_general(
        by_c[...], by_z[...], (((1,), (1,)), ((), ())), preferred_element_type=F32
    ).astype(BF16)


def gram_product(by_c, by_z):
    side = by_c.shape[0]
    vmem = pl.BlockSpec(memory_space=pltpu.VMEM)
    return pl.pallas_call(
        gram_kernel,
        out_shape=jax.ShapeDtypeStruct((side, side), BF16),
        in_specs=[vmem, vmem],
        out_specs=vmem,
        compiler_params=pltpu.CompilerParams(vmem_limit_bytes=24 * 2**20),
    )(by_c, by_z)


def polynomial_kernel(order, gram, right, *refs):
    *left, out = refs
    total = -4.775 * gram[...].astype(F32)
    squared = jnp.zeros_like(total)
    for i, block in enumerate(left):
        squared += jnp.dot(block[...], right[order[i]], preferred_element_type=F32)
    out[...] = (total + 2.0315 * squared).astype(BF16)


def polynomial_product(order, gram, right, left):
    vmem = pl.BlockSpec(memory_space=pltpu.VMEM)
    return pl.pallas_call(
        polynomial_kernel,
        out_shape=jax.ShapeDtypeStruct(gram.shape, BF16),
        in_specs=[pl.BlockSpec(memory_space=pltpu.SMEM)] + [vmem] * (2 + len(left)),
        out_specs=vmem,
        compiler_params=pltpu.CompilerParams(vmem_limit_bytes=32 * 2**20),
    )(order, gram, right, *left)


def sum_kernel(index, mine, *refs):
    *got, near, away = refs
    x = index[0]

    def total(i):
        value = mine[i].astype(F32)
        for block in got:
            value += block[i].astype(F32)
        return value

    near[...] = total(x)
    away[...] = total(1 - x).astype(BF16)


def sum_blocks(x, mine, got):
    vmem = pl.BlockSpec(memory_space=pltpu.VMEM)
    shape = mine.shape[1:]
    return pl.pallas_call(
        sum_kernel,
        out_shape=[jax.ShapeDtypeStruct(shape, F32), jax.ShapeDtypeStruct(shape, BF16)],
        in_specs=[pl.BlockSpec(memory_space=pltpu.SMEM)] + [vmem] * (1 + len(got)),
        out_specs=[vmem, vmem],
        compiler_params=pltpu.CompilerParams(vmem_limit_bytes=32 * 2**20),
    )(x.reshape(1).astype(jnp.int32), mine, *got)


def body(iterate):
    row = lax.axis_index("row")
    x, z, y = row // NZ, row % NZ, lax.axis_index("col")
    rows = iterate.shape[0]
    side = NZ * rows

    def z_at(k):
        return (z + k) % NZ

    def c_at(dx, dy):
        return ((x + dx) % NX) * NY + (y + dy) % NY

    def pick(value, index):
        return lax.dynamic_index_in_dim(value, index, 0, keepdims=False)

    plus, minus = Lane(), Lane()
    cut = COLS * 3 // 4
    other = plus.send(iterate, x_swap)
    own_a = minus.send(iterate, y_shift, -1)
    own_b = plus.send(iterate, y_shift, 1)
    other_a = minus.send(other, y_shift, -1)
    other_b = plus.send(other, y_shift, 1)
    own_l = minus.send(own_a[:, :cut], y_shift, -1)
    own_r = plus.send(own_b[:, cut:], y_shift, 1)
    other_l = minus.send(other_a[:, :cut], y_shift, -1)
    other_r = plus.send(other_b[:, cut:], y_shift, 1)
    by_z = jnp.zeros((NZ, rows, COLS), BF16)
    for k, block in gather_z(iterate, 1).items():
        by_z = place(by_z, block, z_at(k), 1)
    by_c = jnp.zeros((NX * NY, rows, COLS), BF16)
    for dx, blocks in enumerate(
        ((iterate, own_a, own_b, (own_l, own_r)), (other, other_a, other_b, (other_l, other_r)))
    ):
        for k, block in zip((0, 1, 3, 2), blocks):
            by_c = place(by_c, block, c_at(dx, k), 1)
    by_z, by_c = by_z.reshape(side, COLS), by_c.reshape(side, COLS)

    gram = gram_product(by_c, by_z)

    half = side // 2
    z1, z7, other, own1, own3 = sent = together(
        [(gram, z_shift, -1), (gram, z_shift, 1), (gram, x_swap), (gram, y_shift, -1), (gram, y_shift, 1)]
    )
    pair = jnp.stack([gram, other])
    z2, z6 = together([(z1, z_shift, -1), (z7, z_shift, 1)], (z1, z7, other))
    other1, other3, pair2 = together(
        [(other, y_shift, -1), (other, y_shift, 1), (pair, y_shift, 2)], (own1, own3)
    )
    z3, z5 = z_shift(z2, -1), z_shift(z6, 1)
    low, high = z_shift(z3[:half], -1), z_shift(z5[half:], 1)
    left = {(0, 0): gram, (0, 1): own1, (0, 2): pair2[0], (0, 3): own3}
    left |= {(1, 0): other, (1, 1): other1, (1, 2): pair2[1], (1, 3): other3}
    right = jnp.zeros((NZ, side, side), BF16)
    for k, block in enumerate((gram, z1, z2, z3, (low, high), z5, z6, z7)):
        right = place(right, block, z_at(k), 0)
    right = lax.optimization_barrier(right)
    right = right.reshape(NZ, NX * NY, rows, side).swapaxes(0, 1).reshape(NX * NY, side, side)
    order = jnp.stack([c_at(dx, k) for dx, k in left]).astype(jnp.int32)
    polynomial = polynomial_product(order, gram, right, list(left.values()))
    polynomial_t = polynomial.T

    def add(term, got):
        return (term.astype(F32) + got.astype(F32)).astype(BF16)

    far = NZ // 2
    for_z = jnp.dot(polynomial_t, by_c[:, SPLIT:], preferred_element_type=F32).astype(BF16)
    polynomial, _ = lax.optimization_barrier((polynomial, for_z))
    for_z = for_z.reshape(NZ, rows, COLS - SPLIT)
    for_c = jnp.dot(polynomial, by_z[:, :SPLIT], preferred_element_type=F32).astype(BF16)
    for_c = for_c.reshape(NX, NY, rows, SPLIT)

    def term_z(k):
        return pick(for_z, z_at(k))

    def term_c(k):
        return lax.dynamic_index_in_dim(for_c, (y + k) % NY, 1, keepdims=False)

    far_term = term_z(far)
    half = far_term.shape[1] // 2
    up, down = z_shift(far_term[:, :half], 1), z_shift(far_term[:, half:], -1)
    got_c = [y_shift(term_c(k), k) for k in (2, 1, 3)]
    a, b = term_z(far - 1), term_z(1 - far)
    a = jnp.concatenate([add(a[:, :half], up), a[:, half:]], 1)
    b = jnp.concatenate([b[:, :half], add(b[:, half:], down)], 1)
    a, b, _ = lax.optimization_barrier((a, b, for_c))
    up, down = z_shift(a, 1), z_shift(b, -1)
    up, down = together(
        [(add(term_z(2), up), z_shift, 1), (add(term_z(-2), down), z_shift, -1)], (up, down)
    )
    sum_c, away = sum_blocks(x, term_c(0), got_c)
    up, down = together(
        [(add(term_z(1), up), z_shift, 1), (add(term_z(-1), down), z_shift, -1)], (up, down)
    )
    first = x_swap(away[:, :FIRST])
    second, _ = lax.optimization_barrier((away[:, FIRST:], first))
    got_x = jnp.concatenate([first, x_swap(second)], 1)
    sum_z = term_z(0).astype(F32) + up.astype(F32) + down.astype(F32)
    sum_c = sum_c + got_x.astype(F32)
    update = 3.4445 * iterate.astype(F32) + jnp.concatenate([sum_c, sum_z], 1)
    return (math.sqrt(COLS) * update).astype(BF16)


def solution(mesh):
    return jax.shard_map(
        body,
        mesh=mesh,
        in_specs=(P(("mat", "row", "col"), None),),
        out_specs=P(("mat", "row", "col"), None),
        check_vma=False,
    )
```

```python
import math

import jax
import jax.numpy as jnp
from jax import lax
from jax.experimental import pallas as pl
from jax.experimental.pallas import tpu as pltpu
from jax.sharding import PartitionSpec as P

COLS = 9216
SPLIT = 3328
BLOCK = 4608
FIRST = 256
NX, NZ, NY = 2, 8, 4
F32, BF16 = jnp.float32, jnp.bfloat16


def z_shift(value, step):
    pairs = [(x * NZ + z, x * NZ + (z + step) % NZ) for x in range(NX) for z in range(NZ)]
    return lax.ppermute(value, "row", pairs)


def x_swap(value):
    pairs = [(x * NZ + z, (1 - x) * NZ + z) for x in range(NX) for z in range(NZ)]
    return lax.ppermute(value, "row", pairs)


def y_shift(value, step):
    return lax.ppermute(value, "col", [(y, (y + step) % NY) for y in range(NY)])


def together(sends, after=None):
    values, _ = lax.optimization_barrier(([send[0] for send in sends], after))
    return [send[1](value, *send[2:]) for value, send in zip(values, sends)]


class Lane:
    def __init__(self):
        self.last = None

    def send(self, value, shift, *step):
        if self.last is not None:
            value, _ = lax.optimization_barrier((value, self.last))
        self.last = shift(value, *step)
        return self.last


def gather_z(block, axis):
    half = block.shape[axis] // 2
    blocks = {0: block}
    ahead = behind = block
    for step in range(1, NZ // 2):
        ahead, behind = z_shift(ahead, -1), z_shift(behind, 1)
        blocks[step], blocks[NZ - step] = ahead, behind
    left = z_shift(lax.slice_in_dim(ahead, 0, half, axis=axis), -1)
    right = z_shift(lax.slice_in_dim(behind, half, 2 * half, axis=axis), 1)
    blocks[NZ // 2] = (left, right)
    return blocks


def place(buffer, block, index, axis):
    if isinstance(block, tuple):
        left, right = block
        buffer = lax.dynamic_update_slice(buffer, left[None], (index, 0, 0))
        start = (index, left.shape[0], 0) if axis == 0 else (index, 0, left.shape[1])
        return lax.dynamic_update_slice(buffer, right[None], start)
    return lax.dynamic_update_slice(buffer, block[None], (index, 0, 0))


def gram_kernel(by_c, by_z, out, total):
    step = pl.program_id(0)

    @pl.when(step == 0)
    def _():
        total[...] = jnp.zeros_like(total)

    total[...] += lax.dot_general(
        by_c[...], by_z[...], (((1,), (1,)), ((), ())), preferred_element_type=F32
    )

    @pl.when(step == pl.num_programs(0) - 1)
    def _():
        out[...] = total[...].astype(BF16)


def gram_product(by_c, by_z):
    side = by_c.shape[0]
    block = pl.BlockSpec((side, BLOCK), lambda k: (0, k))
    return pl.pallas_call(
        gram_kernel,
        out_shape=jax.ShapeDtypeStruct((side, side), BF16),
        grid=(COLS // BLOCK,),
        in_specs=[block, block],
        out_specs=pl.BlockSpec((side, side), lambda k: (0, 0)),
        scratch_shapes=[pltpu.VMEM((side, side), F32)],
        compiler_params=pltpu.CompilerParams(vmem_limit_bytes=48 * 2**20),
    )(by_c, by_z)


def polynomial_kernel(order, gram, right, *refs):
    *left, out = refs
    total = -4.775 * gram[...].astype(F32)
    squared = jnp.zeros_like(total)
    for i, block in enumerate(left):
        squared += jnp.dot(block[...], right[order[i]], preferred_element_type=F32)
    out[...] = (total + 2.0315 * squared).astype(BF16)


def polynomial_product(order, gram, right, left):
    vmem = pl.BlockSpec(memory_space=pltpu.VMEM)
    return pl.pallas_call(
        polynomial_kernel,
        out_shape=jax.ShapeDtypeStruct(gram.shape, BF16),
        in_specs=[pl.BlockSpec(memory_space=pltpu.SMEM)] + [vmem] * (2 + len(left)),
        out_specs=vmem,
        compiler_params=pltpu.CompilerParams(vmem_limit_bytes=32 * 2**20),
    )(order, gram, right, *left)


def sum_kernel(index, mine, *refs):
    *got, near, away = refs
    x = index[0]

    def total(i):
        value = mine[i].astype(F32)
        for block in got:
            value += block[i].astype(F32)
        return value

    near[...] = total(x)
    away[...] = total(1 - x).astype(BF16)


def sum_blocks(x, mine, got):
    vmem = pl.BlockSpec(memory_space=pltpu.VMEM)
    shape = mine.shape[1:]
    return pl.pallas_call(
        sum_kernel,
        out_shape=[jax.ShapeDtypeStruct(shape, F32), jax.ShapeDtypeStruct(shape, BF16)],
        in_specs=[pl.BlockSpec(memory_space=pltpu.SMEM)] + [vmem] * (1 + len(got)),
        out_specs=[vmem, vmem],
        compiler_params=pltpu.CompilerParams(vmem_limit_bytes=32 * 2**20),
    )(x.reshape(1).astype(jnp.int32), mine, *got)


def body(iterate):
    row = lax.axis_index("row")
    x, z, y = row // NZ, row % NZ, lax.axis_index("col")
    rows = iterate.shape[0]
    side = NZ * rows

    def z_at(k):
        return (z + k) % NZ

    def c_at(dx, dy):
        return ((x + dx) % NX) * NY + (y + dy) % NY

    def pick(value, index):
        return lax.dynamic_index_in_dim(value, index, 0, keepdims=False)

    plus, minus = Lane(), Lane()
    cut = COLS * 3 // 4
    other = plus.send(iterate, x_swap)
    own_a = minus.send(iterate, y_shift, -1)
    own_b = plus.send(iterate, y_shift, 1)
    other_a = minus.send(other, y_shift, -1)
    other_b = plus.send(other, y_shift, 1)
    own_l = minus.send(own_a[:, :cut], y_shift, -1)
    own_r = plus.send(own_b[:, cut:], y_shift, 1)
    other_l = minus.send(other_a[:, :cut], y_shift, -1)
    other_r = plus.send(other_b[:, cut:], y_shift, 1)
    by_z = jnp.zeros((NZ, rows, COLS), BF16)
    for k, block in gather_z(iterate, 1).items():
        by_z = place(by_z, block, z_at(k), 1)
    by_c = jnp.zeros((NX * NY, rows, COLS), BF16)
    for dx, blocks in enumerate(
        ((iterate, own_a, own_b, (own_l, own_r)), (other, other_a, other_b, (other_l, other_r)))
    ):
        for k, block in zip((0, 1, 3, 2), blocks):
            by_c = place(by_c, block, c_at(dx, k), 1)
    by_z, by_c = by_z.reshape(side, COLS), by_c.reshape(side, COLS)

    gram = gram_product(by_c, by_z)

    half = side // 2
    z1, z7, other, own1, own3 = sent = together(
        [(gram, z_shift, -1), (gram, z_shift, 1), (gram, x_swap), (gram, y_shift, -1), (gram, y_shift, 1)]
    )
    pair = jnp.stack([gram, other])
    z2, z6 = together([(z1, z_shift, -1), (z7, z_shift, 1)], (z1, z7, other))
    other1, other3, pair2 = together(
        [(other, y_shift, -1), (other, y_shift, 1), (pair, y_shift, 2)], (own1, own3)
    )
    z3, z5 = z_shift(z2, -1), z_shift(z6, 1)
    low, high = z_shift(z3[:half], -1), z_shift(z5[half:], 1)
    left = {(0, 0): gram, (0, 1): own1, (0, 2): pair2[0], (0, 3): own3}
    left |= {(1, 0): other, (1, 1): other1, (1, 2): pair2[1], (1, 3): other3}
    right = jnp.zeros((NZ, side, side), BF16)
    for k, block in enumerate((gram, z1, z2, z3, (low, high), z5, z6, z7)):
        right = place(right, block, z_at(k), 0)
    right = lax.optimization_barrier(right)
    right = right.reshape(NZ, NX * NY, rows, side).swapaxes(0, 1).reshape(NX * NY, side, side)
    order = jnp.stack([c_at(dx, k) for dx, k in left]).astype(jnp.int32)
    polynomial = polynomial_product(order, gram, right, list(left.values()))
    polynomial_t = polynomial.T

    def add(term, got):
        return (term.astype(F32) + got.astype(F32)).astype(BF16)

    far = NZ // 2
    for_z = jnp.dot(polynomial_t, by_c[:, SPLIT:], preferred_element_type=F32).astype(BF16)
    polynomial, _ = lax.optimization_barrier((polynomial, for_z))
    for_z = for_z.reshape(NZ, rows, COLS - SPLIT)
    for_c = jnp.dot(polynomial, by_z[:, :SPLIT], preferred_element_type=F32).astype(BF16)
    for_c = for_c.reshape(NX, NY, rows, SPLIT)

    def term_z(k):
        return pick(for_z, z_at(k))

    def term_c(k):
        return lax.dynamic_index_in_dim(for_c, (y + k) % NY, 1, keepdims=False)

    far_term = term_z(far)
    half = far_term.shape[1] // 2
    up, down = z_shift(far_term[:, :half], 1), z_shift(far_term[:, half:], -1)
    got_c = [y_shift(term_c(k), k) for k in (2, 1, 3)]
    a, b = term_z(far - 1), term_z(1 - far)
    a = jnp.concatenate([add(a[:, :half], up), a[:, half:]], 1)
    b = jnp.concatenate([b[:, :half], add(b[:, half:], down)], 1)
    a, b, _ = lax.optimization_barrier((a, b, for_c))
    up, down = z_shift(a, 1), z_shift(b, -1)
    up, down = together(
        [(add(term_z(2), up), z_shift, 1), (add(term_z(-2), down), z_shift, -1)], (up, down)
    )
    sum_c, away = sum_blocks(x, term_c(0), got_c)
    up, down = together(
        [(add(term_z(1), up), z_shift, 1), (add(term_z(-1), down), z_shift, -1)], (up, down)
    )
    first = x_swap(away[:, :FIRST])
    second, _ = lax.optimization_barrier((away[:, FIRST:], first))
    got_x = jnp.concatenate([first, x_swap(second)], 1)
    sum_z = term_z(0).astype(F32) + up.astype(F32) + down.astype(F32)
    sum_c = sum_c + got_x.astype(F32)
    update = 3.4445 * iterate.astype(F32) + jnp.concatenate([sum_c, sum_z], 1)
    return (math.sqrt(COLS) * update).astype(BF16)


def solution(mesh):
    return jax.shard_map(
        body,
        mesh=mesh,
        in_specs=(P(("mat", "row", "col"), None),),
        out_specs=P(("mat", "row", "col"), None),
        check_vma=False,
    )
```

```python
import math

import jax
import jax.numpy as jnp
from jax import lax
from jax.experimental import pallas as pl
from jax.experimental.pallas import tpu as pltpu
from jax.sharding import PartitionSpec as P

COLS = 9216
SPLIT = 3328
BLOCK = 4608
FIRST = 256
NX, NZ, NY = 2, 8, 4
F32, BF16 = jnp.float32, jnp.bfloat16


def z_shift(value, step):
    pairs = [(x * NZ + z, x * NZ + (z + step) % NZ) for x in range(NX) for z in range(NZ)]
    return lax.ppermute(value, "row", pairs)


def x_swap(value):
    pairs = [(x * NZ + z, (1 - x) * NZ + z) for x in range(NX) for z in range(NZ)]
    return lax.ppermute(value, "row", pairs)


def y_shift(value, step):
    return lax.ppermute(value, "col", [(y, (y + step) % NY) for y in range(NY)])


def together(sends, after=None):
    values, _ = lax.optimization_barrier(([send[0] for send in sends], after))
    return [send[1](value, *send[2:]) for value, send in zip(values, sends)]


class Lane:
    def __init__(self):
        self.last = None

    def send(self, value, shift, *step):
        if self.last is not None:
            value, _ = lax.optimization_barrier((value, self.last))
        self.last = shift(value, *step)
        return self.last


def gather_z(block, axis):
    half = block.shape[axis] // 2
    blocks = {0: block}
    ahead = behind = block
    for step in range(1, NZ // 2):
        ahead, behind = z_shift(ahead, -1), z_shift(behind, 1)
        blocks[step], blocks[NZ - step] = ahead, behind
    left = z_shift(lax.slice_in_dim(ahead, 0, half, axis=axis), -1)
    right = z_shift(lax.slice_in_dim(behind, half, 2 * half, axis=axis), 1)
    blocks[NZ // 2] = (left, right)
    return blocks


def place(buffer, block, index, axis):
    if isinstance(block, tuple):
        left, right = block
        buffer = lax.dynamic_update_slice(buffer, left[None], (index, 0, 0))
        start = (index, left.shape[0], 0) if axis == 0 else (index, 0, left.shape[1])
        return lax.dynamic_update_slice(buffer, right[None], start)
    return lax.dynamic_update_slice(buffer, block[None], (index, 0, 0))


def gram_kernel(by_c, by_z, out, total):
    step = pl.program_id(0)

    @pl.when(step == 0)
    def _():
        total[...] = jnp.zeros_like(total)

    total[...] += lax.dot_general(
        by_c[...], by_z[...], (((1,), (1,)), ((), ())), preferred_element_type=F32
    )

    @pl.when(step == pl.num_programs(0) - 1)
    def _():
        out[...] = total[...].astype(BF16)


def gram_product(by_c, by_z):
    side = by_c.shape[0]
    block = pl.BlockSpec((side, BLOCK), lambda k: (0, k))
    return pl.pallas_call(
        gram_kernel,
        out_shape=jax.ShapeDtypeStruct((side, side), BF16),
        grid=(COLS // BLOCK,),
        in_specs=[block, block],
        out_specs=pl.BlockSpec((side, side), lambda k: (0, 0)),
        scratch_shapes=[pltpu.VMEM((side, side), F32)],
        compiler_params=pltpu.CompilerParams(vmem_limit_bytes=48 * 2**20),
    )(by_c, by_z)


def polynomial_kernel(order, gram, right, *refs):
    *left, out = refs
    total = -4.775 * gram[...].astype(F32)
    squared = jnp.zeros_like(total)
    for i, block in enumerate(left):
        squared += jnp.dot(block[...], right[order[i]], preferred_element_type=F32)
    out[...] = (total + 2.0315 * squared).astype(BF16)


def polynomial_product(order, gram, right, left):
    vmem = pl.BlockSpec(memory_space=pltpu.VMEM)
    return pl.pallas_call(
        polynomial_kernel,
        out_shape=jax.ShapeDtypeStruct(gram.shape, BF16),
        in_specs=[pl.BlockSpec(memory_space=pltpu.SMEM)] + [vmem] * (2 + len(left)),
        out_specs=vmem,
        compiler_params=pltpu.CompilerParams(vmem_limit_bytes=32 * 2**20),
    )(order, gram, right, *left)


def sum_kernel(index, mine, *refs):
    *got, near, away = refs
    x = index[0]

    def total(i):
        value = mine[i].astype(F32)
        for block in got:
            value += block[i].astype(F32)
        return value

    near[...] = total(x)
    away[...] = total(1 - x).astype(BF16)


def sum_blocks(x, mine, got):
    vmem = pl.BlockSpec(memory_space=pltpu.VMEM)
    shape = mine.shape[1:]
    return pl.pallas_call(
        sum_kernel,
        out_shape=[jax.ShapeDtypeStruct(shape, F32), jax.ShapeDtypeStruct(shape, BF16)],
        in_specs=[pl.BlockSpec(memory_space=pltpu.SMEM)] + [vmem] * (1 + len(got)),
        out_specs=[vmem, vmem],
        compiler_params=pltpu.CompilerParams(vmem_limit_bytes=32 * 2**20),
    )(x.reshape(1).astype(jnp.int32), mine, *got)


def body(iterate):
    row = lax.axis_index("row")
    x, z, y = row // NZ, row % NZ, lax.axis_index("col")
    rows = iterate.shape[0]
    side = NZ * rows

    def z_at(k):
        return (z + k) % NZ

    def c_at(dx, dy):
        return ((x + dx) % NX) * NY + (y + dy) % NY

    def pick(value, index):
        return lax.dynamic_index_in_dim(value, index, 0, keepdims=False)

    plus, minus = Lane(), Lane()
    cut = COLS * 3 // 4
    other = plus.send(iterate, x_swap)
    own_a = minus.send(iterate, y_shift, -1)
    own_b = plus.send(iterate, y_shift, 1)
    other_a = minus.send(other, y_shift, -1)
    other_b = plus.send(other, y_shift, 1)
    own_l = minus.send(own_a[:, :cut], y_shift, -1)
    own_r = plus.send(own_b[:, cut:], y_shift, 1)
    other_l = minus.send(other_a[:, :cut], y_shift, -1)
    other_r = plus.send(other_b[:, cut:], y_shift, 1)
    by_z = jnp.zeros((NZ, rows, COLS), BF16)
    for k, block in gather_z(iterate, 1).items():
        by_z = place(by_z, block, z_at(k), 1)
    by_c = jnp.zeros((NX * NY, rows, COLS), BF16)
    for dx, blocks in enumerate(
        ((iterate, own_a, own_b, (own_l, own_r)), (other, other_a, other_b, (other_l, other_r)))
    ):
        for k, block in zip((0, 1, 3, 2), blocks):
            by_c = place(by_c, block, c_at(dx, k), 1)
    by_z, by_c = by_z.reshape(side, COLS), by_c.reshape(side, COLS)

    gram = gram_product(by_c, by_z)

    half = side // 2
    z1, z7, other, own1, own3 = sent = together(
        [(gram, z_shift, -1), (gram, z_shift, 1), (gram, x_swap), (gram, y_shift, -1), (gram, y_shift, 1)]
    )
    pair = jnp.stack([gram, other])
    z2, z6 = together([(z1, z_shift, -1), (z7, z_shift, 1)], (z1, z7, other))
    other1, other3, pair2 = together(
        [(other, y_shift, -1), (other, y_shift, 1), (pair, y_shift, 2)], (own1, own3, z2, z6)
    )
    z3, z5 = together([(z2, z_shift, -1), (z6, z_shift, 1)], (z2, z6))
    low, high = z_shift(z3[:half], -1), z_shift(z5[half:], 1)
    left = {(0, 0): gram, (0, 1): own1, (0, 2): pair2[0], (0, 3): own3}
    left |= {(1, 0): other, (1, 1): other1, (1, 2): pair2[1], (1, 3): other3}
    right = jnp.zeros((NZ, side, side), BF16)
    for k, block in enumerate((gram, z1, z2, z3, (low, high), z5, z6, z7)):
        right = place(right, block, z_at(k), 0)
    right = lax.optimization_barrier(right)
    right = right.reshape(NZ, NX * NY, rows, side).swapaxes(0, 1).reshape(NX * NY, side, side)
    order = jnp.stack([c_at(dx, k) for dx, k in left]).astype(jnp.int32)
    polynomial = polynomial_product(order, gram, right, list(left.values()))
    polynomial_t = polynomial.T

    def add(term, got):
        return (term.astype(F32) + got.astype(F32)).astype(BF16)

    far = NZ // 2
    for_z = jnp.dot(polynomial_t, by_c[:, SPLIT:], preferred_element_type=F32).astype(BF16)
    polynomial, _ = lax.optimization_barrier((polynomial, for_z))
    for_z = for_z.reshape(NZ, rows, COLS - SPLIT)
    for_c = jnp.dot(polynomial, by_z[:, :SPLIT], preferred_element_type=F32).astype(BF16)
    for_c = for_c.reshape(NX, NY, rows, SPLIT)

    def term_z(k):
        return pick(for_z, z_at(k))

    def term_c(k):
        return lax.dynamic_index_in_dim(for_c, (y + k) % NY, 1, keepdims=False)

    far_term = term_z(far)
    half = far_term.shape[1] // 2
    up, down = z_shift(far_term[:, :half], 1), z_shift(far_term[:, half:], -1)
    got_c = [y_shift(term_c(k), k) for k in (2, 1, 3)]
    a, b = term_z(far - 1), term_z(1 - far)
    a = jnp.concatenate([add(a[:, :half], up), a[:, half:]], 1)
    b = jnp.concatenate([b[:, :half], add(b[:, half:], down)], 1)
    a, b, _ = lax.optimization_barrier((a, b, for_c))
    up, down = z_shift(a, 1), z_shift(b, -1)
    up, down = together(
        [(add(term_z(2), up), z_shift, 1), (add(term_z(-2), down), z_shift, -1)], (up, down)
    )
    sum_c, away = sum_blocks(x, term_c(0), got_c)
    up, down = together(
        [(add(term_z(1), up), z_shift, 1), (add(term_z(-1), down), z_shift, -1)], (up, down)
    )
    first = x_swap(away[:, :FIRST])
    second, _ = lax.optimization_barrier((away[:, FIRST:], first))
    got_x = jnp.concatenate([first, x_swap(second)], 1)
    sum_z = term_z(0).astype(F32) + up.astype(F32) + down.astype(F32)
    sum_c = sum_c + got_x.astype(F32)
    update = 3.4445 * iterate.astype(F32) + jnp.concatenate([sum_c, sum_z], 1)
    return (math.sqrt(COLS) * update).astype(BF16)


def solution(mesh):
    return jax.shard_map(
        body,
        mesh=mesh,
        in_specs=(P(("mat", "row", "col"), None),),
        out_specs=P(("mat", "row", "col"), None),
        check_vma=False,
    )
```

```python
import math

import jax
import jax.numpy as jnp
from jax import lax
from jax.experimental import pallas as pl
from jax.experimental.pallas import tpu as pltpu
from jax.sharding import PartitionSpec as P

COLS = 9216
SPLIT = 3584
BLOCK = 4608
FIRST = 256
NX, NZ, NY = 2, 8, 4
F32, BF16 = jnp.float32, jnp.bfloat16


def z_shift(value, step):
    pairs = [(x * NZ + z, x * NZ + (z + step) % NZ) for x in range(NX) for z in range(NZ)]
    return lax.ppermute(value, "row", pairs)


def x_swap(value):
    pairs = [(x * NZ + z, (1 - x) * NZ + z) for x in range(NX) for z in range(NZ)]
    return lax.ppermute(value, "row", pairs)


def y_shift(value, step):
    return lax.ppermute(value, "col", [(y, (y + step) % NY) for y in range(NY)])


def together(sends, after=None):
    values, _ = lax.optimization_barrier(([send[0] for send in sends], after))
    return [send[1](value, *send[2:]) for value, send in zip(values, sends)]


class Lane:
    def __init__(self):
        self.last = None

    def send(self, value, shift, *step):
        if self.last is not None:
            value, _ = lax.optimization_barrier((value, self.last))
        self.last = shift(value, *step)
        return self.last


def gather_z(block, axis):
    half = block.shape[axis] // 2
    blocks = {0: block}
    ahead = behind = block
    for step in range(1, NZ // 2):
        ahead, behind = z_shift(ahead, -1), z_shift(behind, 1)
        blocks[step], blocks[NZ - step] = ahead, behind
    left = z_shift(lax.slice_in_dim(ahead, 0, half, axis=axis), -1)
    right = z_shift(lax.slice_in_dim(behind, half, 2 * half, axis=axis), 1)
    blocks[NZ // 2] = (left, right)
    return blocks


def place(buffer, block, index, axis):
    if isinstance(block, tuple):
        left, right = block
        buffer = lax.dynamic_update_slice(buffer, left[None], (index, 0, 0))
        start = (index, left.shape[0], 0) if axis == 0 else (index, 0, left.shape[1])
        return lax.dynamic_update_slice(buffer, right[None], start)
    return lax.dynamic_update_slice(buffer, block[None], (index, 0, 0))


def gram_kernel(by_c, by_z, out, total):
    step = pl.program_id(0)

    @pl.when(step == 0)
    def _():
        total[...] = jnp.zeros_like(total)

    total[...] += lax.dot_general(
        by_c[...], by_z[...], (((1,), (1,)), ((), ())), preferred_element_type=F32
    )

    @pl.when(step == pl.num_programs(0) - 1)
    def _():
        out[...] = total[...].astype(BF16)


def gram_product(by_c, by_z):
    side = by_c.shape[0]
    block = pl.BlockSpec((side, BLOCK), lambda k: (0, k))
    return pl.pallas_call(
        gram_kernel,
        out_shape=jax.ShapeDtypeStruct((side, side), BF16),
        grid=(COLS // BLOCK,),
        in_specs=[block, block],
        out_specs=pl.BlockSpec((side, side), lambda k: (0, 0)),
        scratch_shapes=[pltpu.VMEM((side, side), F32)],
        compiler_params=pltpu.CompilerParams(vmem_limit_bytes=48 * 2**20),
    )(by_c, by_z)


def polynomial_kernel(order, gram, right, *refs):
    *left, out = refs
    total = -4.775 * gram[...].astype(F32)
    squared = jnp.zeros_like(total)
    for i, block in enumerate(left):
        squared += jnp.dot(block[...], right[order[i]], preferred_element_type=F32)
    out[...] = (total + 2.0315 * squared).astype(BF16)


def polynomial_product(order, gram, right, left):
    vmem = pl.BlockSpec(memory_space=pltpu.VMEM)
    return pl.pallas_call(
        polynomial_kernel,
        out_shape=jax.ShapeDtypeStruct(gram.shape, BF16),
        in_specs=[pl.BlockSpec(memory_space=pltpu.SMEM)] + [vmem] * (2 + len(left)),
        out_specs=vmem,
        compiler_params=pltpu.CompilerParams(vmem_limit_bytes=32 * 2**20),
    )(order, gram, right, *left)


def sum_kernel(index, mine, *refs):
    *got, near, away = refs
    x = index[0]

    def total(i):
        value = mine[i].astype(F32)
        for block in got:
            value += block[i].astype(F32)
        return value

    near[...] = total(x)
    away[...] = total(1 - x).astype(BF16)


def sum_blocks(x, mine, got):
    vmem = pl.BlockSpec(memory_space=pltpu.VMEM)
    shape = mine.shape[1:]
    return pl.pallas_call(
        sum_kernel,
        out_shape=[jax.ShapeDtypeStruct(shape, F32), jax.ShapeDtypeStruct(shape, BF16)],
        in_specs=[pl.BlockSpec(memory_space=pltpu.SMEM)] + [vmem] * (1 + len(got)),
        out_specs=[vmem, vmem],
        compiler_params=pltpu.CompilerParams(vmem_limit_bytes=32 * 2**20),
    )(x.reshape(1).astype(jnp.int32), mine, *got)


def pair_kernel(*refs):
    terms, got, out = refs[:2], refs[2:4], refs[4:]
    for i in range(2):
        out[i][...] = (terms[i][...].astype(F32) + got[i][...].astype(F32)).astype(BF16)


def add_pair(terms, got):
    vmem = pl.BlockSpec(memory_space=pltpu.VMEM)
    shape = jax.ShapeDtypeStruct(terms[0].shape, BF16)
    return pl.pallas_call(
        pair_kernel,
        out_shape=[shape, shape],
        in_specs=[vmem] * 4,
        out_specs=[vmem, vmem],
        compiler_params=pltpu.CompilerParams(vmem_limit_bytes=16 * 2**20),
    )(*terms, *got)


def body(iterate):
    row = lax.axis_index("row")
    x, z, y = row // NZ, row % NZ, lax.axis_index("col")
    rows = iterate.shape[0]
    side = NZ * rows

    def z_at(k):
        return (z + k) % NZ

    def c_at(dx, dy):
        return ((x + dx) % NX) * NY + (y + dy) % NY

    def pick(value, index):
        return lax.dynamic_index_in_dim(value, index, 0, keepdims=False)

    plus, minus = Lane(), Lane()
    cut = COLS * 3 // 4
    other = plus.send(iterate, x_swap)
    own_a = minus.send(iterate, y_shift, -1)
    own_b = plus.send(iterate, y_shift, 1)
    other_a = minus.send(other, y_shift, -1)
    other_b = plus.send(other, y_shift, 1)
    own_l = minus.send(own_a[:, :cut], y_shift, -1)
    own_r = plus.send(own_b[:, cut:], y_shift, 1)
    other_l = minus.send(other_a[:, :cut], y_shift, -1)
    other_r = plus.send(other_b[:, cut:], y_shift, 1)
    by_z = jnp.zeros((NZ, rows, COLS), BF16)
    for k, block in gather_z(iterate, 1).items():
        by_z = place(by_z, block, z_at(k), 1)
    by_c = jnp.zeros((NX * NY, rows, COLS), BF16)
    for dx, blocks in enumerate(
        ((iterate, own_a, own_b, (own_l, own_r)), (other, other_a, other_b, (other_l, other_r)))
    ):
        for k, block in zip((0, 1, 3, 2), blocks):
            by_c = place(by_c, block, c_at(dx, k), 1)
    by_z, by_c = by_z.reshape(side, COLS), by_c.reshape(side, COLS)

    gram = gram_product(by_c, by_z)

    half = side // 2
    z1, z7, other, own1, own3 = sent = together(
        [(gram, z_shift, -1), (gram, z_shift, 1), (gram, x_swap), (gram, y_shift, -1), (gram, y_shift, 1)]
    )
    pair = jnp.stack([gram, other])
    z2, z6 = together([(z1, z_shift, -1), (z7, z_shift, 1)], (z1, z7, other))
    other1, other3, pair2 = together(
        [(other, y_shift, -1), (other, y_shift, 1), (pair, y_shift, 2)], (own1, own3)
    )
    z3, z5 = z_shift(z2, -1), z_shift(z6, 1)
    low, high = z_shift(z3[:half], -1), z_shift(z5[half:], 1)
    left = {(0, 0): gram, (0, 1): own1, (0, 2): pair2[0], (0, 3): own3}
    left |= {(1, 0): other, (1, 1): other1, (1, 2): pair2[1], (1, 3): other3}
    right = jnp.zeros((NZ, side, side), BF16)
    for k, block in enumerate((gram, z1, z2, z3, (low, high), z5, z6, z7)):
        right = place(right, block, z_at(k), 0)
    right = lax.optimization_barrier(right)
    right = right.reshape(NZ, NX * NY, rows, side).swapaxes(0, 1).reshape(NX * NY, side, side)
    order = jnp.stack([c_at(dx, k) for dx, k in left]).astype(jnp.int32)
    polynomial = polynomial_product(order, gram, right, list(left.values()))
    polynomial_t = polynomial.T

    def add(term, got):
        return (term.astype(F32) + got.astype(F32)).astype(BF16)

    far = NZ // 2
    for_z = jnp.dot(polynomial_t, by_c[:, SPLIT:], preferred_element_type=F32).astype(BF16)
    polynomial, _ = lax.optimization_barrier((polynomial, for_z))
    for_z = for_z.reshape(NZ, rows, COLS - SPLIT)
    for_c = jnp.dot(polynomial, by_z[:, :SPLIT], preferred_element_type=F32).astype(BF16)
    for_c = for_c.reshape(NX, NY, rows, SPLIT)

    def term_z(k):
        return pick(for_z, z_at(k))

    def term_c(k):
        return lax.dynamic_index_in_dim(for_c, (y + k) % NY, 1, keepdims=False)

    far_term = term_z(far)
    half = far_term.shape[1] // 2
    up, down = z_shift(far_term[:, :half], 1), z_shift(far_term[:, half:], -1)
    later = {k: term_z(k) for k in (2, -2, 1, -1, 0)}
    got_c = [y_shift(term_c(k), k) for k in (2, 1, 3)]
    a, b = term_z(far - 1), term_z(1 - far)
    a = jnp.concatenate([add(a[:, :half], up), a[:, half:]], 1)
    b = jnp.concatenate([b[:, :half], add(b[:, half:], down)], 1)
    a, b, _ = lax.optimization_barrier((a, b, for_c))
    up, down = z_shift(a, 1), z_shift(b, -1)
    a, b = add_pair((later[2], later[-2]), (up, down))
    up, down = z_shift(a, 1), z_shift(b, -1)
    sum_c, away = sum_blocks(x, term_c(0), got_c)
    a, b = add_pair((later[1], later[-1]), (up, down))
    up, down = z_shift(a, 1), z_shift(b, -1)
    first = x_swap(away[:, :FIRST])
    second, _ = lax.optimization_barrier((away[:, FIRST:], first))
    got_x = jnp.concatenate([first, x_swap(second)], 1)
    sum_z = later[0].astype(F32) + up.astype(F32) + down.astype(F32)
    sum_c = sum_c + got_x.astype(F32)
    update = 3.4445 * iterate.astype(F32) + jnp.concatenate([sum_c, sum_z], 1)
    return (math.sqrt(COLS) * update).astype(BF16)


def solution(mesh):
    return jax.shard_map(
        body,
        mesh=mesh,
        in_specs=(P(("mat", "row", "col"), None),),
        out_specs=P(("mat", "row", "col"), None),
        check_vma=False,
    )
```

```python
import math

import jax
import jax.numpy as jnp
from jax import lax
from jax.experimental import pallas as pl
from jax.experimental.pallas import tpu as pltpu
from jax.sharding import PartitionSpec as P

COLS = 9216
SPLIT = 3328
BLOCK = 4608
FIRST = 256
NX, NZ, NY = 2, 8, 4
F32, BF16 = jnp.float32, jnp.bfloat16


def z_shift(value, step):
    pairs = [(x * NZ + z, x * NZ + (z + step) % NZ) for x in range(NX) for z in range(NZ)]
    return lax.ppermute(value, "row", pairs)


def x_swap(value):
    pairs = [(x * NZ + z, (1 - x) * NZ + z) for x in range(NX) for z in range(NZ)]
    return lax.ppermute(value, "row", pairs)


def y_shift(value, step):
    return lax.ppermute(value, "col", [(y, (y + step) % NY) for y in range(NY)])


def together(sends, after=None):
    values, _ = lax.optimization_barrier(([send[0] for send in sends], after))
    return [send[1](value, *send[2:]) for value, send in zip(values, sends)]


class Lane:
    def __init__(self):
        self.last = None

    def send(self, value, shift, *step):
        if self.last is not None:
            value, _ = lax.optimization_barrier((value, self.last))
        self.last = shift(value, *step)
        return self.last


def gather_z(block, axis):
    half = block.shape[axis] // 2
    blocks = {0: block}
    ahead = behind = block
    for step in range(1, NZ // 2):
        ahead, behind = z_shift(ahead, -1), z_shift(behind, 1)
        blocks[step], blocks[NZ - step] = ahead, behind
    left = z_shift(lax.slice_in_dim(ahead, 0, half, axis=axis), -1)
    right = z_shift(lax.slice_in_dim(behind, half, 2 * half, axis=axis), 1)
    blocks[NZ // 2] = (left, right)
    return blocks


def place(buffer, block, index, axis):
    if isinstance(block, tuple):
        left, right = block
        buffer = lax.dynamic_update_slice(buffer, left[None], (index, 0, 0))
        start = (index, left.shape[0], 0) if axis == 0 else (index, 0, left.shape[1])
        return lax.dynamic_update_slice(buffer, right[None], start)
    return lax.dynamic_update_slice(buffer, block[None], (index, 0, 0))


def gram_kernel(by_c, by_z, out, total):
    step = pl.program_id(0)

    @pl.when(step == 0)
    def _():
        total[...] = jnp.zeros_like(total)

    total[...] += lax.dot_general(
        by_c[...], by_z[...], (((1,), (1,)), ((), ())), preferred_element_type=F32
    )

    @pl.when(step == pl.num_programs(0) - 1)
    def _():
        out[...] = total[...].astype(BF16)


def gram_product(by_c, by_z):
    side = by_c.shape[0]
    block = pl.BlockSpec((side, BLOCK), lambda k: (0, k))
    return pl.pallas_call(
        gram_kernel,
        out_shape=jax.ShapeDtypeStruct((side, side), BF16),
        grid=(COLS // BLOCK,),
        in_specs=[block, block],
        out_specs=pl.BlockSpec((side, side), lambda k: (0, 0)),
        scratch_shapes=[pltpu.VMEM((side, side), F32)],
        compiler_params=pltpu.CompilerParams(vmem_limit_bytes=48 * 2**20),
    )(by_c, by_z)


def polynomial_kernel(order, gram, right, *refs):
    *left, out = refs
    total = -4.775 * gram[...].astype(F32)
    squared = jnp.zeros_like(total)
    for i, block in enumerate(left):
        squared += jnp.dot(block[...], right[order[i]], preferred_element_type=F32)
    out[...] = (total + 2.0315 * squared).astype(BF16)


def polynomial_product(order, gram, right, left):
    vmem = pl.BlockSpec(memory_space=pltpu.VMEM)
    return pl.pallas_call(
        polynomial_kernel,
        out_shape=jax.ShapeDtypeStruct(gram.shape, BF16),
        in_specs=[pl.BlockSpec(memory_space=pltpu.SMEM)] + [vmem] * (2 + len(left)),
        out_specs=vmem,
        compiler_params=pltpu.CompilerParams(vmem_limit_bytes=32 * 2**20),
    )(order, gram, right, *left)


def sum_kernel(index, mine, *refs):
    *got, near, away = refs
    x = index[0]

    def total(i):
        value = mine[i].astype(F32)
        for block in got:
            value += block[i].astype(F32)
        return value

    near[...] = total(x)
    away[...] = total(1 - x).astype(BF16)


def sum_blocks(x, mine, got):
    vmem = pl.BlockSpec(memory_space=pltpu.VMEM)
    shape = mine.shape[1:]
    return pl.pallas_call(
        sum_kernel,
        out_shape=[jax.ShapeDtypeStruct(shape, F32), jax.ShapeDtypeStruct(shape, BF16)],
        in_specs=[pl.BlockSpec(memory_space=pltpu.SMEM)] + [vmem] * (1 + len(got)),
        out_specs=[vmem, vmem],
        compiler_params=pltpu.CompilerParams(vmem_limit_bytes=32 * 2**20),
    )(x.reshape(1).astype(jnp.int32), mine, *got)


def pair_kernel(*refs):
    terms, got, out = refs[:2], refs[2:4], refs[4:]
    for i in range(2):
        out[i][...] = (terms[i][...].astype(F32) + got[i][...].astype(F32)).astype(BF16)


def add_pair(terms, got):
    vmem = pl.BlockSpec(memory_space=pltpu.VMEM)
    shape = jax.ShapeDtypeStruct(terms[0].shape, BF16)
    return pl.pallas_call(
        pair_kernel,
        out_shape=[shape, shape],
        in_specs=[vmem] * 4,
        out_specs=[vmem, vmem],
        compiler_params=pltpu.CompilerParams(vmem_limit_bytes=16 * 2**20),
    )(*terms, *got)


def body(iterate):
    row = lax.axis_index("row")
    x, z, y = row // NZ, row % NZ, lax.axis_index("col")
    rows = iterate.shape[0]
    side = NZ * rows

    def z_at(k):
        return (z + k) % NZ

    def c_at(dx, dy):
        return ((x + dx) % NX) * NY + (y + dy) % NY

    def pick(value, index):
        return lax.dynamic_index_in_dim(value, index, 0, keepdims=False)

    plus, minus = Lane(), Lane()
    cut = COLS * 3 // 4
    other = plus.send(iterate, x_swap)
    own_a = minus.send(iterate, y_shift, -1)
    own_b = plus.send(iterate, y_shift, 1)
    other_a = minus.send(other, y_shift, -1)
    other_b = plus.send(other, y_shift, 1)
    own_l = minus.send(own_a[:, :cut], y_shift, -1)
    own_r = plus.send(own_b[:, cut:], y_shift, 1)
    other_l = minus.send(other_a[:, :cut], y_shift, -1)
    other_r = plus.send(other_b[:, cut:], y_shift, 1)
    by_z = jnp.zeros((NZ, rows, COLS), BF16)
    for k, block in gather_z(iterate, 1).items():
        by_z = place(by_z, block, z_at(k), 1)
    by_c = jnp.zeros((NX * NY, rows, COLS), BF16)
    for dx, blocks in enumerate(
        ((iterate, own_a, own_b, (own_l, own_r)), (other, other_a, other_b, (other_l, other_r)))
    ):
        for k, block in zip((0, 1, 3, 2), blocks):
            by_c = place(by_c, block, c_at(dx, k), 1)
    by_z, by_c = by_z.reshape(side, COLS), by_c.reshape(side, COLS)

    gram = gram_product(by_c, by_z)

    half = side // 2
    z1, z7, other, own1, own3 = sent = together(
        [(gram, z_shift, -1), (gram, z_shift, 1), (gram, x_swap), (gram, y_shift, -1), (gram, y_shift, 1)]
    )
    pair = jnp.stack([gram, other])
    z2, z6 = together([(z1, z_shift, -1), (z7, z_shift, 1)], (z1, z7, other))
    other1, other3, pair2 = together(
        [(other, y_shift, -1), (other, y_shift, 1), (pair, y_shift, 2)], (own1, own3)
    )
    z3, z5 = z_shift(z2, -1), z_shift(z6, 1)
    low, high = z_shift(z3[:half], -1), z_shift(z5[half:], 1)
    left = {(0, 0): gram, (0, 1): own1, (0, 2): pair2[0], (0, 3): own3}
    left |= {(1, 0): other, (1, 1): other1, (1, 2): pair2[1], (1, 3): other3}
    right = jnp.zeros((NZ, side, side), BF16)
    for k, block in enumerate((gram, z1, z2, z3, (low, high), z5, z6, z7)):
        right = place(right, block, z_at(k), 0)
    right = lax.optimization_barrier(right)
    right = right.reshape(NZ, NX * NY, rows, side).swapaxes(0, 1).reshape(NX * NY, side, side)
    order = jnp.stack([c_at(dx, k) for dx, k in left]).astype(jnp.int32)
    polynomial = polynomial_product(order, gram, right, list(left.values()))
    polynomial_t = polynomial.T

    def add(term, got):
        return (term.astype(F32) + got.astype(F32)).astype(BF16)

    far = NZ // 2
    for_z = jnp.dot(polynomial_t, by_c[:, SPLIT:], preferred_element_type=F32).astype(BF16)
    polynomial, _ = lax.optimization_barrier((polynomial, for_z))
    for_z = for_z.reshape(NZ, rows, COLS - SPLIT)
    for_c = jnp.dot(polynomial, by_z[:, :SPLIT], preferred_element_type=F32).astype(BF16)
    for_c = for_c.reshape(NX, NY, rows, SPLIT)

    def term_z(k):
        return pick(for_z, z_at(k))

    def term_c(k):
        return lax.dynamic_index_in_dim(for_c, (y + k) % NY, 1, keepdims=False)

    far_term = term_z(far)
    half = far_term.shape[1] // 2
    up, down = z_shift(far_term[:, :half], 1), z_shift(far_term[:, half:], -1)
    later = {k: term_z(k) for k in (2, -2, 1, -1, 0)}
    got_c = [y_shift(term_c(k), k) for k in (2, 1, 3)]
    a, b = term_z(far - 1), term_z(1 - far)
    a = jnp.concatenate([add(a[:, :half], up), a[:, half:]], 1)
    b = jnp.concatenate([b[:, :half], add(b[:, half:], down)], 1)
    a, b, _ = lax.optimization_barrier((a, b, for_c))
    up, down = z_shift(a, 1), z_shift(b, -1)
    a, b = add_pair((later[2], later[-2]), (up, down))
    up, down = z_shift(a, 1), z_shift(b, -1)
    sum_c, away = sum_blocks(x, term_c(0), got_c)
    a, b = add_pair((later[1], later[-1]), (up, down))
    up, down = z_shift(a, 1), z_shift(b, -1)
    first = x_swap(away[:, :FIRST])
    second, _ = lax.optimization_barrier((away[:, FIRST:], (first, a, b)))
    got_x = jnp.concatenate([first, x_swap(second)], 1)
    sum_z = later[0].astype(F32) + up.astype(F32) + down.astype(F32)
    sum_c = sum_c + got_x.astype(F32)
    update = 3.4445 * iterate.astype(F32) + jnp.concatenate([sum_c, sum_z], 1)
    return (math.sqrt(COLS) * update).astype(BF16)


def solution(mesh):
    return jax.shard_map(
        body,
        mesh=mesh,
        in_specs=(P(("mat", "row", "col"), None),),
        out_specs=P(("mat", "row", "col"), None),
        check_vma=False,
    )
```

```python
import math

import jax
import jax.numpy as jnp
from jax import lax
from jax.experimental import pallas as pl
from jax.experimental.pallas import tpu as pltpu
from jax.sharding import PartitionSpec as P

COLS = 9216
SPLIT = 3584
BLOCK = 4608
FIRST = 256
NX, NZ, NY = 2, 8, 4
F32, BF16 = jnp.float32, jnp.bfloat16


def z_shift(value, step):
    pairs = [(x * NZ + z, x * NZ + (z + step) % NZ) for x in range(NX) for z in range(NZ)]
    return lax.ppermute(value, "row", pairs)


def x_swap(value):
    pairs = [(x * NZ + z, (1 - x) * NZ + z) for x in range(NX) for z in range(NZ)]
    return lax.ppermute(value, "row", pairs)


def y_shift(value, step):
    return lax.ppermute(value, "col", [(y, (y + step) % NY) for y in range(NY)])


def together(sends, after=None):
    values, _ = lax.optimization_barrier(([send[0] for send in sends], after))
    return [send[1](value, *send[2:]) for value, send in zip(values, sends)]


class Lane:
    def __init__(self):
        self.last = None

    def send(self, value, shift, *step):
        if self.last is not None:
            value, _ = lax.optimization_barrier((value, self.last))
        self.last = shift(value, *step)
        return self.last


def gather_z(block, axis):
    half = block.shape[axis] // 2
    blocks = {0: block}
    ahead = behind = block
    for step in range(1, NZ // 2):
        ahead, behind = z_shift(ahead, -1), z_shift(behind, 1)
        blocks[step], blocks[NZ - step] = ahead, behind
    left = z_shift(lax.slice_in_dim(ahead, 0, half, axis=axis), -1)
    right = z_shift(lax.slice_in_dim(behind, half, 2 * half, axis=axis), 1)
    blocks[NZ // 2] = (left, right)
    return blocks


def place(buffer, block, index, axis):
    if isinstance(block, tuple):
        left, right = block
        buffer = lax.dynamic_update_slice(buffer, left[None], (index, 0, 0))
        start = (index, left.shape[0], 0) if axis == 0 else (index, 0, left.shape[1])
        return lax.dynamic_update_slice(buffer, right[None], start)
    return lax.dynamic_update_slice(buffer, block[None], (index, 0, 0))


def gram_kernel(by_c, by_z, out, total):
    step = pl.program_id(0)

    @pl.when(step == 0)
    def _():
        total[...] = jnp.zeros_like(total)

    total[...] += lax.dot_general(
        by_c[...], by_z[...], (((1,), (1,)), ((), ())), preferred_element_type=F32
    )

    @pl.when(step == pl.num_programs(0) - 1)
    def _():
        out[...] = total[...].astype(BF16)


def gram_product(by_c, by_z):
    side = by_c.shape[0]
    block = pl.BlockSpec((side, BLOCK), lambda k: (0, k))
    return pl.pallas_call(
        gram_kernel,
        out_shape=jax.ShapeDtypeStruct((side, side), BF16),
        grid=(COLS // BLOCK,),
        in_specs=[block, block],
        out_specs=pl.BlockSpec((side, side), lambda k: (0, 0)),
        scratch_shapes=[pltpu.VMEM((side, side), F32)],
        compiler_params=pltpu.CompilerParams(vmem_limit_bytes=22 * 2**20),
    )(by_c, by_z)


def polynomial_kernel(order, gram, right, *refs):
    *left, out = refs
    total = -4.775 * gram[...].astype(F32)
    squared = jnp.zeros_like(total)
    for i, block in enumerate(left):
        squared += jnp.dot(block[...], right[order[i]], preferred_element_type=F32)
    out[...] = (total + 2.0315 * squared).astype(BF16)


def polynomial_product(order, gram, right, left):
    vmem = pl.BlockSpec(memory_space=pltpu.VMEM)
    return pl.pallas_call(
        polynomial_kernel,
        out_shape=jax.ShapeDtypeStruct(gram.shape, BF16),
        in_specs=[pl.BlockSpec(memory_space=pltpu.SMEM)] + [vmem] * (2 + len(left)),
        out_specs=vmem,
        compiler_params=pltpu.CompilerParams(vmem_limit_bytes=16 * 2**20),
    )(order, gram, right, *left)


def sum_kernel(index, mine, *refs):
    *got, near, away = refs
    x = index[0]

    def total(i):
        value = mine[i].astype(F32)
        for block in got:
            value += block[i].astype(F32)
        return value

    near[...] = total(x)
    away[...] = total(1 - x).astype(BF16)


def sum_blocks(x, mine, got):
    vmem = pl.BlockSpec(memory_space=pltpu.VMEM)
    shape = mine.shape[1:]
    return pl.pallas_call(
        sum_kernel,
        out_shape=[jax.ShapeDtypeStruct(shape, F32), jax.ShapeDtypeStruct(shape, BF16)],
        in_specs=[pl.BlockSpec(memory_space=pltpu.SMEM)] + [vmem] * (1 + len(got)),
        out_specs=[vmem, vmem],
        compiler_params=pltpu.CompilerParams(vmem_limit_bytes=12 * 2**20),
    )(x.reshape(1).astype(jnp.int32), mine, *got)


def pair_kernel(*refs):
    terms, got, out = refs[:2], refs[2:4], refs[4:]
    for i in range(2):
        out[i][...] = (terms[i][...].astype(F32) + got[i][...].astype(F32)).astype(BF16)


def add_pair(terms, got):
    vmem = pl.BlockSpec(memory_space=pltpu.VMEM)
    shape = jax.ShapeDtypeStruct(terms[0].shape, BF16)
    return pl.pallas_call(
        pair_kernel,
        out_shape=[shape, shape],
        in_specs=[vmem] * 4,
        out_specs=[vmem, vmem],
        compiler_params=pltpu.CompilerParams(vmem_limit_bytes=12 * 2**20),
    )(*terms, *got)


def body(iterate):
    row = lax.axis_index("row")
    x, z, y = row // NZ, row % NZ, lax.axis_index("col")
    rows = iterate.shape[0]
    side = NZ * rows

    def z_at(k):
        return (z + k) % NZ

    def c_at(dx, dy):
        return ((x + dx) % NX) * NY + (y + dy) % NY

    def pick(value, index):
        return lax.dynamic_index_in_dim(value, index, 0, keepdims=False)

    plus, minus = Lane(), Lane()
    cut = COLS * 3 // 4
    other = plus.send(iterate, x_swap)
    own_a = minus.send(iterate, y_shift, -1)
    own_b = plus.send(iterate, y_shift, 1)
    other_a = minus.send(other, y_shift, -1)
    other_b = plus.send(other, y_shift, 1)
    own_l = minus.send(own_a[:, :cut], y_shift, -1)
    own_r = plus.send(own_b[:, cut:], y_shift, 1)
    other_l = minus.send(other_a[:, :cut], y_shift, -1)
    other_r = plus.send(other_b[:, cut:], y_shift, 1)
    by_z = jnp.zeros((NZ, rows, COLS), BF16)
    for k, block in gather_z(iterate, 1).items():
        by_z = place(by_z, block, z_at(k), 1)
    by_c = jnp.zeros((NX * NY, rows, COLS), BF16)
    for dx, blocks in enumerate(
        ((iterate, own_a, own_b, (own_l, own_r)), (other, other_a, other_b, (other_l, other_r)))
    ):
        for k, block in zip((0, 1, 3, 2), blocks):
            by_c = place(by_c, block, c_at(dx, k), 1)
    by_z, by_c = by_z.reshape(side, COLS), by_c.reshape(side, COLS)

    gram = gram_product(by_c, by_z)

    half = side // 2
    z1, z7, other, own1, own3 = sent = together(
        [(gram, z_shift, -1), (gram, z_shift, 1), (gram, x_swap), (gram, y_shift, -1), (gram, y_shift, 1)]
    )
    pair = jnp.stack([gram, other])
    z2, z6 = together([(z1, z_shift, -1), (z7, z_shift, 1)], (z1, z7, other))
    other1, other3, pair2 = together(
        [(other, y_shift, -1), (other, y_shift, 1), (pair, y_shift, 2)], (own1, own3)
    )
    z3, z5 = z_shift(z2, -1), z_shift(z6, 1)
    low, high = z_shift(z3[:half], -1), z_shift(z5[half:], 1)
    left = {(0, 0): gram, (0, 1): own1, (0, 2): pair2[0], (0, 3): own3}
    left |= {(1, 0): other, (1, 1): other1, (1, 2): pair2[1], (1, 3): other3}
    right = jnp.zeros((NZ, side, side), BF16)
    for k, block in enumerate((gram, z1, z2, z3, (low, high), z5, z6, z7)):
        right = place(right, block, z_at(k), 0)
    right = lax.optimization_barrier(right)
    right = right.reshape(NZ, NX * NY, rows, side).swapaxes(0, 1).reshape(NX * NY, side, side)
    order = jnp.stack([c_at(dx, k) for dx, k in left]).astype(jnp.int32)
    polynomial = polynomial_product(order, gram, right, list(left.values()))
    polynomial_t = polynomial.T

    def add(term, got):
        return (term.astype(F32) + got.astype(F32)).astype(BF16)

    far = NZ // 2
    for_z = jnp.dot(polynomial_t, by_c[:, SPLIT:], preferred_element_type=F32).astype(BF16)
    polynomial, _ = lax.optimization_barrier((polynomial, for_z))
    for_z = for_z.reshape(NZ, rows, COLS - SPLIT)
    for_c = jnp.dot(polynomial, by_z[:, :SPLIT], preferred_element_type=F32).astype(BF16)
    for_c = for_c.reshape(NX, NY, rows, SPLIT)

    def term_z(k):
        return pick(for_z, z_at(k))

    def term_c(k):
        return lax.dynamic_index_in_dim(for_c, (y + k) % NY, 1, keepdims=False)

    far_term = term_z(far)
    half = far_term.shape[1] // 2
    up, down = z_shift(far_term[:, :half], 1), z_shift(far_term[:, half:], -1)
    later = {k: term_z(k) for k in (2, -2, 1, -1, 0)}
    got_c = [y_shift(term_c(k), k) for k in (2, 1, 3)]
    a, b = term_z(far - 1), term_z(1 - far)
    a = jnp.concatenate([add(a[:, :half], up), a[:, half:]], 1)
    b = jnp.concatenate([b[:, :half], add(b[:, half:], down)], 1)
    a, b, _ = lax.optimization_barrier((a, b, for_c))
    up, down = z_shift(a, 1), z_shift(b, -1)
    a, b = add_pair((later[2], later[-2]), (up, down))
    up, down = z_shift(a, 1), z_shift(b, -1)
    sum_c, away = sum_blocks(x, term_c(0), got_c)
    a, b = add_pair((later[1], later[-1]), (up, down))
    up, down = z_shift(a, 1), z_shift(b, -1)
    first = x_swap(away[:, :FIRST])
    second, _ = lax.optimization_barrier((away[:, FIRST:], first))
    got_x = jnp.concatenate([first, x_swap(second)], 1)
    sum_z = later[0].astype(F32) + up.astype(F32) + down.astype(F32)
    sum_c = sum_c + got_x.astype(F32)
    update = 3.4445 * iterate.astype(F32) + jnp.concatenate([sum_c, sum_z], 1)
    return (math.sqrt(COLS) * update).astype(BF16)


def solution(mesh):
    return jax.shard_map(
        body,
        mesh=mesh,
        in_specs=(P(("mat", "row", "col"), None),),
        out_specs=P(("mat", "row", "col"), None),
        check_vma=False,
    )
```

```python
import math

import jax
import jax.numpy as jnp
from jax import lax
from jax.experimental import pallas as pl
from jax.experimental.pallas import tpu as pltpu
from jax.sharding import PartitionSpec as P

COLS = 9216
SPLIT = 4096
BLOCK = 4608
FIRST = 256
NX, NZ, NY = 2, 8, 4
F32, BF16 = jnp.float32, jnp.bfloat16


def z_shift(value, step):
    pairs = [(x * NZ + z, x * NZ + (z + step) % NZ) for x in range(NX) for z in range(NZ)]
    return lax.ppermute(value, "row", pairs)


def x_swap(value):
    pairs = [(x * NZ + z, (1 - x) * NZ + z) for x in range(NX) for z in range(NZ)]
    return lax.ppermute(value, "row", pairs)


def y_shift(value, step):
    return lax.ppermute(value, "col", [(y, (y + step) % NY) for y in range(NY)])


def together(sends, after=None):
    values, _ = lax.optimization_barrier(([send[0] for send in sends], after))
    return [send[1](value, *send[2:]) for value, send in zip(values, sends)]


class Lane:
    def __init__(self):
        self.last = None

    def send(self, value, shift, *step):
        if self.last is not None:
            value, _ = lax.optimization_barrier((value, self.last))
        self.last = shift(value, *step)
        return self.last


def gather_z(block, axis):
    half = block.shape[axis] // 2
    blocks = {0: block}
    ahead = behind = block
    for step in range(1, NZ // 2):
        ahead, behind = z_shift(ahead, -1), z_shift(behind, 1)
        blocks[step], blocks[NZ - step] = ahead, behind
    left = z_shift(lax.slice_in_dim(ahead, 0, half, axis=axis), -1)
    right = z_shift(lax.slice_in_dim(behind, half, 2 * half, axis=axis), 1)
    blocks[NZ // 2] = (left, right)
    return blocks


def place(buffer, block, index, axis):
    if isinstance(block, tuple):
        left, right = block
        buffer = lax.dynamic_update_slice(buffer, left[None], (index, 0, 0))
        start = (index, left.shape[0], 0) if axis == 0 else (index, 0, left.shape[1])
        return lax.dynamic_update_slice(buffer, right[None], start)
    return lax.dynamic_update_slice(buffer, block[None], (index, 0, 0))


def gram_kernel(by_c, by_z, out, total):
    step = pl.program_id(0)

    @pl.when(step == 0)
    def _():
        total[...] = jnp.zeros_like(total)

    total[...] += lax.dot_general(
        by_c[...], by_z[...], (((1,), (1,)), ((), ())), preferred_element_type=F32
    )

    @pl.when(step == pl.num_programs(0) - 1)
    def _():
        out[...] = total[...].astype(BF16)


def gram_product(by_c, by_z):
    side = by_c.shape[0]
    block = pl.BlockSpec((side, BLOCK), lambda k: (0, k))
    return pl.pallas_call(
        gram_kernel,
        out_shape=jax.ShapeDtypeStruct((side, side), BF16),
        grid=(COLS // BLOCK,),
        in_specs=[block, block],
        out_specs=pl.BlockSpec((side, side), lambda k: (0, 0)),
        scratch_shapes=[pltpu.VMEM((side, side), F32)],
        compiler_params=pltpu.CompilerParams(vmem_limit_bytes=48 * 2**20),
    )(by_c, by_z)


def polynomial_kernel(order, gram, right, *refs):
    *left, out = refs
    total = -4.775 * gram[...].astype(F32)
    squared = jnp.zeros_like(total)
    for i, block in enumerate(left):
        squared += jnp.dot(block[...], right[order[i]], preferred_element_type=F32)
    out[...] = (total + 2.0315 * squared).astype(BF16)


def polynomial_product(order, gram, right, left):
    vmem = pl.BlockSpec(memory_space=pltpu.VMEM)
    return pl.pallas_call(
        polynomial_kernel,
        out_shape=jax.ShapeDtypeStruct(gram.shape, BF16),
        in_specs=[pl.BlockSpec(memory_space=pltpu.SMEM)] + [vmem] * (2 + len(left)),
        out_specs=vmem,
        compiler_params=pltpu.CompilerParams(vmem_limit_bytes=32 * 2**20),
    )(order, gram, right, *left)


def sum_kernel(index, mine, *refs):
    *got, near, away = refs
    x = index[0]

    def total(i):
        value = mine[i].astype(F32)
        for block in got:
            value += block[i].astype(F32)
        return value

    near[...] = total(x)
    away[...] = total(1 - x).astype(BF16)


def sum_blocks(x, mine, got):
    vmem = pl.BlockSpec(memory_space=pltpu.VMEM)
    shape = mine.shape[1:]
    return pl.pallas_call(
        sum_kernel,
        out_shape=[jax.ShapeDtypeStruct(shape, F32), jax.ShapeDtypeStruct(shape, BF16)],
        in_specs=[pl.BlockSpec(memory_space=pltpu.SMEM)] + [vmem] * (1 + len(got)),
        out_specs=[vmem, vmem],
        compiler_params=pltpu.CompilerParams(vmem_limit_bytes=32 * 2**20),
    )(x.reshape(1).astype(jnp.int32), mine, *got)


def pair_kernel(*refs):
    terms, got, out = refs[:2], refs[2:4], refs[4:]
    for i in range(2):
        out[i][...] = (terms[i][...].astype(F32) + got[i][...].astype(F32)).astype(BF16)


def add_pair(terms, got):
    vmem = pl.BlockSpec(memory_space=pltpu.VMEM)
    shape = jax.ShapeDtypeStruct(terms[0].shape, BF16)
    return pl.pallas_call(
        pair_kernel,
        out_shape=[shape, shape],
        in_specs=[vmem] * 4,
        out_specs=[vmem, vmem],
        compiler_params=pltpu.CompilerParams(vmem_limit_bytes=16 * 2**20),
    )(*terms, *got)


def body(iterate):
    row = lax.axis_index("row")
    x, z, y = row // NZ, row % NZ, lax.axis_index("col")
    rows = iterate.shape[0]
    side = NZ * rows

    def z_at(k):
        return (z + k) % NZ

    def c_at(dx, dy):
        return ((x + dx) % NX) * NY + (y + dy) % NY

    def pick(value, index):
        return lax.dynamic_index_in_dim(value, index, 0, keepdims=False)

    plus, minus = Lane(), Lane()
    cut = COLS * 3 // 4
    other = plus.send(iterate, x_swap)
    own_a = minus.send(iterate, y_shift, -1)
    own_b = plus.send(iterate, y_shift, 1)
    other_a = minus.send(other, y_shift, -1)
    other_b = plus.send(other, y_shift, 1)
    own_l = minus.send(own_a[:, :cut], y_shift, -1)
    own_r = plus.send(own_b[:, cut:], y_shift, 1)
    other_l = minus.send(other_a[:, :cut], y_shift, -1)
    other_r = plus.send(other_b[:, cut:], y_shift, 1)
    by_z = jnp.zeros((NZ, rows, COLS), BF16)
    for k, block in gather_z(iterate, 1).items():
        by_z = place(by_z, block, z_at(k), 1)
    by_c = jnp.zeros((NX * NY, rows, COLS), BF16)
    for dx, blocks in enumerate(
        ((iterate, own_a, own_b, (own_l, own_r)), (other, other_a, other_b, (other_l, other_r)))
    ):
        for k, block in zip((0, 1, 3, 2), blocks):
            by_c = place(by_c, block, c_at(dx, k), 1)
    by_z, by_c = by_z.reshape(side, COLS), by_c.reshape(side, COLS)

    gram = gram_product(by_c, by_z)

    half = side // 2
    z1, z7, other, own1, own3 = sent = together(
        [(gram, z_shift, -1), (gram, z_shift, 1), (gram, x_swap), (gram, y_shift, -1), (gram, y_shift, 1)]
    )
    pair = jnp.stack([gram, other])
    z2, z6 = together([(z1, z_shift, -1), (z7, z_shift, 1)], (z1, z7, other))
    other1, other3, pair2 = together(
        [(other, y_shift, -1), (other, y_shift, 1), (pair, y_shift, 2)], (own1, own3)
    )
    z3, z5 = z_shift(z2, -1), z_shift(z6, 1)
    low, high = z_shift(z3[:half], -1), z_shift(z5[half:], 1)
    left = {(0, 0): gram, (0, 1): own1, (0, 2): pair2[0], (0, 3): own3}
    left |= {(1, 0): other, (1, 1): other1, (1, 2): pair2[1], (1, 3): other3}
    right = jnp.zeros((NZ, side, side), BF16)
    for k, block in enumerate((gram, z1, z2, z3, (low, high), z5, z6, z7)):
        right = place(right, block, z_at(k), 0)
    right = lax.optimization_barrier(right)
    right = right.reshape(NZ, NX * NY, rows, side).swapaxes(0, 1).reshape(NX * NY, side, side)
    order = jnp.stack([c_at(dx, k) for dx, k in left]).astype(jnp.int32)
    polynomial = polynomial_product(order, gram, right, list(left.values()))
    polynomial_t = polynomial.T

    def add(term, got):
        return (term.astype(F32) + got.astype(F32)).astype(BF16)

    far = NZ // 2
    for_c = jnp.dot(polynomial, by_z[:, :SPLIT], preferred_element_type=F32).astype(BF16)
    polynomial_t, for_c = lax.optimization_barrier((polynomial_t, for_c))
    for_c = for_c.reshape(NX, NY, rows, SPLIT)
    for_z = jnp.dot(polynomial_t, by_c[:, SPLIT:], preferred_element_type=F32).astype(BF16)
    for_z = for_z.reshape(NZ, rows, COLS - SPLIT)

    def term_z(k):
        return pick(for_z, z_at(k))

    def term_c(k):
        return lax.dynamic_index_in_dim(for_c, (y + k) % NY, 1, keepdims=False)

    far_term = term_z(far)
    half = far_term.shape[1] // 2
    up, down = z_shift(far_term[:, :half], 1), z_shift(far_term[:, half:], -1)
    later = {k: term_z(k) for k in (2, -2, 1, -1, 0)}
    got_c = [y_shift(term_c(k), k) for k in (2, 1, 3)]
    a, b = term_z(far - 1), term_z(1 - far)
    a = jnp.concatenate([add(a[:, :half], up), a[:, half:]], 1)
    b = jnp.concatenate([b[:, :half], add(b[:, half:], down)], 1)
    a, b, _ = lax.optimization_barrier((a, b, for_c))
    up, down = z_shift(a, 1), z_shift(b, -1)
    a, b = add_pair((later[2], later[-2]), (up, down))
    up, down = z_shift(a, 1), z_shift(b, -1)
    sum_c, away = sum_blocks(x, term_c(0), got_c)
    a, b = add_pair((later[1], later[-1]), (up, down))
    up, down = z_shift(a, 1), z_shift(b, -1)
    first = x_swap(away[:, :FIRST])
    second, _ = lax.optimization_barrier((away[:, FIRST:], first))
    got_x = jnp.concatenate([first, x_swap(second)], 1)
    sum_z = later[0].astype(F32) + up.astype(F32) + down.astype(F32)
    sum_c = sum_c + got_x.astype(F32)
    update = 3.4445 * iterate.astype(F32) + jnp.concatenate([sum_c, sum_z], 1)
    return (math.sqrt(COLS) * update).astype(BF16)


def solution(mesh):
    return jax.shard_map(
        body,
        mesh=mesh,
        in_specs=(P(("mat", "row", "col"), None),),
        out_specs=P(("mat", "row", "col"), None),
        check_vma=False,
    )
```

```python
import math

import jax
import jax.numpy as jnp
from jax import lax
from jax.experimental import pallas as pl
from jax.experimental.pallas import tpu as pltpu
from jax.sharding import PartitionSpec as P

COLS = 9216
SPLIT = 4096
BLOCK = 4608
NX, NZ, NY = 2, 8, 4
F32, BF16 = jnp.float32, jnp.bfloat16


def z_shift(value, step):
    pairs = [(x * NZ + z, x * NZ + (z + step) % NZ) for x in range(NX) for z in range(NZ)]
    return lax.ppermute(value, "row", pairs)


def x_swap(value):
    pairs = [(x * NZ + z, (1 - x) * NZ + z) for x in range(NX) for z in range(NZ)]
    return lax.ppermute(value, "row", pairs)


def y_shift(value, step):
    return lax.ppermute(value, "col", [(y, (y + step) % NY) for y in range(NY)])


def together(sends, after=None):
    values, _ = lax.optimization_barrier(([send[0] for send in sends], after))
    return [send[1](value, *send[2:]) for value, send in zip(values, sends)]


class Lane:
    def __init__(self):
        self.last = None

    def send(self, value, shift, *step):
        if self.last is not None:
            value, _ = lax.optimization_barrier((value, self.last))
        self.last = shift(value, *step)
        return self.last


def gather_z(block, axis):
    half = block.shape[axis] // 2
    blocks = {0: block}
    ahead = behind = block
    for step in range(1, NZ // 2):
        ahead, behind = z_shift(ahead, -1), z_shift(behind, 1)
        blocks[step], blocks[NZ - step] = ahead, behind
    left = z_shift(lax.slice_in_dim(ahead, 0, half, axis=axis), -1)
    right = z_shift(lax.slice_in_dim(behind, half, 2 * half, axis=axis), 1)
    blocks[NZ // 2] = (left, right)
    return blocks


def place(buffer, block, index, axis):
    if isinstance(block, tuple):
        left, right = block
        buffer = lax.dynamic_update_slice(buffer, left[None], (index, 0, 0))
        start = (index, left.shape[0], 0) if axis == 0 else (index, 0, left.shape[1])
        return lax.dynamic_update_slice(buffer, right[None], start)
    return lax.dynamic_update_slice(buffer, block[None], (index, 0, 0))


def gram_kernel(by_c, by_z, out, total):
    step = pl.program_id(0)

    @pl.when(step == 0)
    def _():
        total[...] = jnp.zeros_like(total)

    total[...] += lax.dot_general(
        by_c[...], by_z[...], (((1,), (1,)), ((), ())), preferred_element_type=F32
    )

    @pl.when(step == pl.num_programs(0) - 1)
    def _():
        out[...] = total[...].astype(BF16)


def gram_product(by_c, by_z):
    side = by_c.shape[0]
    block = pl.BlockSpec((side, BLOCK), lambda k: (0, k))
    return pl.pallas_call(
        gram_kernel,
        out_shape=jax.ShapeDtypeStruct((side, side), BF16),
        grid=(COLS // BLOCK,),
        in_specs=[block, block],
        out_specs=pl.BlockSpec((side, side), lambda k: (0, 0)),
        scratch_shapes=[pltpu.VMEM((side, side), F32)],
        compiler_params=pltpu.CompilerParams(vmem_limit_bytes=48 * 2**20),
    )(by_c, by_z)


def polynomial_kernel(order, gram, right, *refs):
    *left, out = refs
    total = -4.775 * gram[...].astype(F32)
    squared = jnp.zeros_like(total)
    for i, block in enumerate(left):
        squared += jnp.dot(block[...], right[order[i]], preferred_element_type=F32)
    out[...] = (total + 2.0315 * squared).astype(BF16)


def polynomial_product(order, gram, right, left):
    vmem = pl.BlockSpec(memory_space=pltpu.VMEM)
    return pl.pallas_call(
        polynomial_kernel,
        out_shape=jax.ShapeDtypeStruct(gram.shape, BF16),
        in_specs=[pl.BlockSpec(memory_space=pltpu.SMEM)] + [vmem] * (2 + len(left)),
        out_specs=vmem,
        compiler_params=pltpu.CompilerParams(vmem_limit_bytes=32 * 2**20),
    )(order, gram, right, *left)


def sum_kernel(index, mine, *refs):
    *got, near, away = refs
    x = index[0]

    def total(i):
        value = mine[i].astype(F32)
        for block in got:
            value += block[i].astype(F32)
        return value

    near[...] = total(x)
    away[...] = total(1 - x).astype(BF16)


def sum_blocks(x, mine, got):
    vmem = pl.BlockSpec(memory_space=pltpu.VMEM)
    shape = mine.shape[1:]
    return pl.pallas_call(
        sum_kernel,
        out_shape=[jax.ShapeDtypeStruct(shape, F32), jax.ShapeDtypeStruct(shape, BF16)],
        in_specs=[pl.BlockSpec(memory_space=pltpu.SMEM)] + [vmem] * (1 + len(got)),
        out_specs=[vmem, vmem],
        compiler_params=pltpu.CompilerParams(vmem_limit_bytes=32 * 2**20),
    )(x.reshape(1).astype(jnp.int32), mine, *got)


def pair_kernel(*refs):
    terms, got, out = refs[:2], refs[2:4], refs[4:]
    for i in range(2):
        out[i][...] = (terms[i][...].astype(F32) + got[i][...].astype(F32)).astype(BF16)


def add_pair(terms, got):
    vmem = pl.BlockSpec(memory_space=pltpu.VMEM)
    shape = jax.ShapeDtypeStruct(terms[0].shape, BF16)
    return pl.pallas_call(
        pair_kernel,
        out_shape=[shape, shape],
        in_specs=[vmem] * 4,
        out_specs=[vmem, vmem],
        compiler_params=pltpu.CompilerParams(vmem_limit_bytes=16 * 2**20),
    )(*terms, *got)


def body(iterate):
    row = lax.axis_index("row")
    x, z, y = row // NZ, row % NZ, lax.axis_index("col")
    rows = iterate.shape[0]
    side = NZ * rows

    def z_at(k):
        return (z + k) % NZ

    def c_at(dx, dy):
        return ((x + dx) % NX) * NY + (y + dy) % NY

    def pick(value, index):
        return lax.dynamic_index_in_dim(value, index, 0, keepdims=False)

    plus, minus = Lane(), Lane()
    cut = COLS * 3 // 4
    other = plus.send(iterate, x_swap)
    own_a = minus.send(iterate, y_shift, -1)
    own_b = plus.send(iterate, y_shift, 1)
    other_a = minus.send(other, y_shift, -1)
    other_b = plus.send(other, y_shift, 1)
    own_l = minus.send(own_a[:, :cut], y_shift, -1)
    own_r = plus.send(own_b[:, cut:], y_shift, 1)
    other_l = minus.send(other_a[:, :cut], y_shift, -1)
    other_r = plus.send(other_b[:, cut:], y_shift, 1)
    by_z = jnp.zeros((NZ, rows, COLS), BF16)
    for k, block in gather_z(iterate, 1).items():
        by_z = place(by_z, block, z_at(k), 1)
    by_c = jnp.zeros((NX * NY, rows, COLS), BF16)
    for dx, blocks in enumerate(
        ((iterate, own_a, own_b, (own_l, own_r)), (other, other_a, other_b, (other_l, other_r)))
    ):
        for k, block in zip((0, 1, 3, 2), blocks):
            by_c = place(by_c, block, c_at(dx, k), 1)
    by_z, by_c = by_z.reshape(side, COLS), by_c.reshape(side, COLS)

    gram = gram_product(by_c, by_z)

    half = side // 2
    z1, z7, other, own1, own3 = sent = together(
        [(gram, z_shift, -1), (gram, z_shift, 1), (gram, x_swap), (gram, y_shift, -1), (gram, y_shift, 1)]
    )
    pair = jnp.stack([gram, other])
    z2, z6 = together([(z1, z_shift, -1), (z7, z_shift, 1)], (z1, z7, other))
    other1, other3, pair2 = together(
        [(other, y_shift, -1), (other, y_shift, 1), (pair, y_shift, 2)], (own1, own3)
    )
    z3, z5 = z_shift(z2, -1), z_shift(z6, 1)
    low, high = z_shift(z3[:half], -1), z_shift(z5[half:], 1)
    left = {(0, 0): gram, (0, 1): own1, (0, 2): pair2[0], (0, 3): own3}
    left |= {(1, 0): other, (1, 1): other1, (1, 2): pair2[1], (1, 3): other3}
    right = jnp.zeros((NZ, side, side), BF16)
    for k, block in enumerate((gram, z1, z2, z3, (low, high), z5, z6, z7)):
        right = place(right, block, z_at(k), 0)
    right = lax.optimization_barrier(right)
    right = right.reshape(NZ, NX * NY, rows, side).swapaxes(0, 1).reshape(NX * NY, side, side)
    order = jnp.stack([c_at(dx, k) for dx, k in left]).astype(jnp.int32)
    polynomial = polynomial_product(order, gram, right, list(left.values()))
    polynomial_t = polynomial.T

    def add(term, got):
        return (term.astype(F32) + got.astype(F32)).astype(BF16)

    far = NZ // 2
    for_c = jnp.dot(polynomial, by_z[:, :SPLIT], preferred_element_type=F32).astype(BF16)
    polynomial_t, for_c = lax.optimization_barrier((polynomial_t, for_c))
    for_c = for_c.reshape(NX, NY, rows, SPLIT)
    for_z = jnp.dot(polynomial_t, by_c[:, SPLIT:], preferred_element_type=F32).astype(BF16)
    for_z = for_z.reshape(NZ, rows, COLS - SPLIT)

    def term_z(k):
        return pick(for_z, z_at(k))

    def term_c(k):
        return lax.dynamic_index_in_dim(for_c, (y + k) % NY, 1, keepdims=False)

    far_term = term_z(far)
    half = far_term.shape[1] // 2
    up, down = z_shift(far_term[:, :half], 1), z_shift(far_term[:, half:], -1)
    later = {k: term_z(k) for k in (2, -2, 1, -1, 0)}
    got_c = [y_shift(term_c(k), k) for k in (2, 1, 3)]
    a, b = term_z(far - 1), term_z(1 - far)
    a = jnp.concatenate([add(a[:, :half], up), a[:, half:]], 1)
    b = jnp.concatenate([b[:, :half], add(b[:, half:], down)], 1)
    a, b, _ = lax.optimization_barrier((a, b, for_c))
    up, down = z_shift(a, 1), z_shift(b, -1)
    a, b = add_pair((later[2], later[-2]), (up, down))
    up, down = z_shift(a, 1), z_shift(b, -1)
    sum_c, away = sum_blocks(x, term_c(0), got_c)
    a, b = add_pair((later[1], later[-1]), (up, down))
    up, down = z_shift(a, 1), z_shift(b, -1)
    got_x = x_swap(away)
    sum_z = later[0].astype(F32) + up.astype(F32) + down.astype(F32)
    sum_c = sum_c + got_x.astype(F32)
    update = 3.4445 * iterate.astype(F32) + jnp.concatenate([sum_c, sum_z], 1)
    return (math.sqrt(COLS) * update).astype(BF16)


def solution(mesh):
    return jax.shard_map(
        body,
        mesh=mesh,
        in_specs=(P(("mat", "row", "col"), None),),
        out_specs=P(("mat", "row", "col"), None),
        check_vma=False,
    )
```
